128 devices in a mesh: rep: 8 (over x, z_hi), fsdp: 16 (over z_lo, y, core).
Axes of the slice: x: 4, y: 4, z: 4 (z_hi: 2, z_lo: 2; z = z_hi * 2 + z_lo), core: 2. Of those that a mesh axis runs over, the one named last changes fastest.
Arguments:
- deltas: bfloat16 [8, 8192, 1024], P('rep', 'fsdp'), may hold values from -3 to 3
- outer_weights: float32 [16, 8, 64, 1024], P('fsdp', 'rep'), may hold values from -6 to 6
- momentum: float32 [16, 8, 64, 1024], P('fsdp', 'rep'), may hold values from -3 to 3
- tokens: bfloat16 [65536, 8192], P(('rep', 'fsdp')), may hold values from -24 to 24
- key_cot: bfloat16 [65536, 1024], P(('rep', 'fsdp')), may hold values from -6 to 6
Outputs:
- new_outer: float32 [16, 8, 64, 1024], P('fsdp', 'rep')
- new_moment: float32 [16, 8, 64, 1024], P('fsdp', 'rep')
- new_weights: bfloat16 [8192, 1024], P('fsdp')
- keys: bfloat16 [65536, 1024], P(('rep', 'fsdp'))
- token_grad: bfloat16 [65536, 8192], P(('rep', 'fsdp'))
- weight_grad: float32 [8, 8192, 1024], P('rep', 'fsdp')
The draws below stay inside these ranges and needn't reach their ends.
All inputs are finite; a program needn't handle non-finite values.
Results may differ from the reference program's by a relative error of at most 0.02.
Values may be sent and summed in bfloat16 or wider, within the bound.
No kernel may reach another device: no remote copies, remote signals or barrier semaphores. Data moves between devices by JAX's collectives and lax.ppermute only.
A program may use at most 192 MiB of HBM per device.

```python
import jax
import jax.numpy as jnp
from jax import lax

D = 8192
TOK_DEV = 512
COLS = 1024
REPLICAS = 8
FSDP_WAYS = 16
ROWS_OWN = 64
TOKENS = 65536


def spiked(values, key, source, target, blocks, factor):
    def block_of(axis_at):
        return (jnp.arange(values.shape[axis_at]) // (values.shape[axis_at] // blocks)).reshape((-1,) + (1,) * (values.ndim - 1 - axis_at))

    near = jax.random.permutation(key, blocks)[block_of(target)]
    far = (block_of(target) + blocks // 2) % blocks
    return jnp.where((block_of(source) == near) | (block_of(source) == far), factor * values, values)


def level_of(rng, shape, shards, smallest, high):
    factor_of, own = 1.0, jax.random.fold_in(rng, 6)
    for axis_at, parts in shards:
        steps = jnp.exp(jax.random.uniform(jax.random.fold_in(own, axis_at), (parts,), jnp.float32, smallest / len(shards), high / len(shards)))
        factor_of = factor_of * jnp.repeat(steps, shape[axis_at] // parts).reshape([-1 if axis == axis_at else 1 for axis in range(len(shape))])
    return factor_of


def noise(stream_key, extent, spread, reach, shards=(), kind=jnp.bfloat16):
    entries = jax.random.normal(stream_key, extent, jnp.float32) * spread
    if len(shards) > 0:
        entries = level_of(stream_key, extent, shards, -0.22, 0.18) * entries
    return jnp.clip(entries, min=-reach, max=reach).astype(kind)


def gaussian_with(key, shape, scale, most, split, heavy, held_as=jnp.bfloat16):
    values = scale * jax.random.normal(key, shape, jnp.float32)
    if split:
        values = values * level_of(key, shape, split, -0.22, 0.18)
    return jnp.clip(spiked(values, jax.random.fold_in(key, 3), *heavy), -most, most).astype(held_as)


def setup_inputs(seed: int = 0) -> dict:
    streams_of = jax.random.split(jax.random.key(seed), 6)
    return {
        "deltas": gaussian_with(streams_of[0], (REPLICAS, D, COLS), 0.5, 3.0, ((0, 8), (1, 16)), (0, 1, 8, 2.0)),
        "outer_weights": noise(streams_of[1], (FSDP_WAYS, REPLICAS, ROWS_OWN, COLS), 1.0, 6.0, ((0, 16), (1, 8)), jnp.float32),
        "momentum": noise(streams_of[2], (FSDP_WAYS, REPLICAS, ROWS_OWN, COLS), 0.5, 3.0, ((0, 16), (1, 8)), jnp.float32),
        "tokens": gaussian_with(streams_of[3], (TOKENS, D), 1.0, 24.0, ((0, 128),), (0, 1, 128, 5.5)),
        "key_cot": noise(streams_of[4], (TOKENS, COLS), 1.0, 6.0, ((0, 128),)),
    }


MOMENTUM_RATE = 0.9
OUTER_RATE = 0.7


def replica_pass(new_weights, unit_scale, tok_rep, cot_rep):
    keys = (jnp.dot(tok_rep, new_weights, preferred_element_type=jnp.float32) * unit_scale).astype(jnp.bfloat16)
    token_grad = (jnp.dot(cot_rep, new_weights.T, preferred_element_type=jnp.float32) * unit_scale).astype(jnp.bfloat16)
    tok_blocks = tok_rep.reshape(FSDP_WAYS, TOK_DEV, D)
    cot_blocks = cot_rep.reshape(FSDP_WAYS, TOK_DEV, COLS)

    def add_block(running, block_pair):
        block_grad = (jnp.dot(block_pair[0].T, block_pair[1], preferred_element_type=jnp.float32) * unit_scale).astype(jnp.bfloat16)
        block_grad = lax.optimization_barrier(block_grad)
        return running + block_grad.astype(jnp.float32), None

    weight_grad, unused = lax.scan(add_block, jnp.zeros((D, COLS), jnp.float32), (tok_blocks, cot_blocks))
    return keys, token_grad, weight_grad


def reference(deltas, outer_weights, momentum, tokens, key_cot):
    mean_delta = (jnp.sum(deltas.astype(jnp.float32), axis=0) / REPLICAS).reshape(outer_weights.shape)
    new_moment = MOMENTUM_RATE * momentum + mean_delta
    new_outer = outer_weights - OUTER_RATE * (mean_delta + MOMENTUM_RATE * new_moment)
    new_weights = new_outer.reshape(D, COLS).astype(jnp.bfloat16)
    unit_scale = D ** -0.5
    tok_reps = tokens.reshape(REPLICAS, FSDP_WAYS * TOK_DEV, D)
    cot_reps = key_cot.reshape(REPLICAS, FSDP_WAYS * TOK_DEV, COLS)
    keys, token_grad, weight_grad = lax.map(lambda pair_in: replica_pass(new_weights, unit_scale, pair_in[0], pair_in[1]), (tok_reps, cot_reps))
    return (new_outer, new_moment, new_weights, keys.reshape(TOKENS, COLS), token_grad.reshape(TOKENS, D), weight_grad)
```

```python
import itertools

import jax
import jax.numpy as jnp
import numpy as np
from jax import lax
from jax.experimental import pallas as pl
from jax.experimental.pallas import tpu as pltpu
from jax.sharding import Mesh, PartitionSpec as P

MOMENTUM_RATE = 0.9
OUTER_RATE = 0.7
AXES = ("x", "zh", "zl", "y", "c")
SIZES = (4, 2, 2, 4, 2)
TOK = 512
D = 8192
COLS = 1024
SCALE = D ** (-0.5)
VMEM = 48 * 1024 * 1024
ANY = pl.BlockSpec(memory_space=pl.ANY)
BF = jnp.bfloat16
F32 = jnp.float32


def permute(value, to):
    pairs = []
    for x, zh, zl, y, c in itertools.product(*[range(n) for n in SIZES]):
        tx, tz, ty, tc = to(x, zh * 2 + zl, y, c)
        tz = tz % 4
        target = (tx % 4, tz // 2, tz % 2, ty % 4, tc % 2)
        pairs.append(
            (
                int(np.ravel_multi_index((x, zh, zl, y, c), SIZES)),
                int(np.ravel_multi_index(target, SIZES)),
            )
        )
    return lax.ppermute(value, AXES, pairs)


def swap_core(value):
    return permute(value, lambda x, z, y, c: (x, z, y, 1 - c))


def ring_x(value):
    return permute(value, lambda x, z, y, c: (x + 1 - 2 * c, z, y, c))


def ring_z(value):
    return permute(value, lambda x, z, y, c: (x, z + 1 - 2 * c, y, c))


def ring_y(value):
    return permute(value, lambda x, z, y, c: (x, z, y + 1 - 2 * c, c))


def params(**more):
    return pltpu.CompilerParams(vmem_limit_bytes=VMEM, **more)


def half_kernel(at, tokens, out, held, in_sem, out_sem):
    c = at[4]
    loads = [
        pltpu.make_async_copy(
            tokens.at[:, pl.ds(pl.multiple_of((2 * g + 1 - c) * 512, 512), 512)],
            held.at[:, pl.ds(g * 512, 512)],
            in_sem.at[g],
        )
        for g in range(8)
    ]
    stores = [
        pltpu.make_async_copy(
            held.at[:, pl.ds(g * 512, 512)],
            out.at[:, pl.ds(g * 512, 512)],
            out_sem.at[g],
        )
        for g in range(8)
    ]
    for load in loads:
        load.start()
    for load, store in zip(loads, stores):
        load.wait()
        store.start()
    for store in stores:
        store.wait()


def other_half(at, tokens):
    return pl.pallas_call(
        half_kernel,
        out_shape=jax.ShapeDtypeStruct((TOK, D // 2), BF),
        in_specs=[pl.BlockSpec(memory_space=pltpu.SMEM), ANY],
        out_specs=ANY,
        scratch_shapes=[
            pltpu.VMEM((TOK, D // 2), BF),
            pltpu.SemaphoreType.DMA((8,)),
            pltpu.SemaphoreType.DMA((8,)),
        ],
        compiler_params=params(),
        cost_estimate=pl.CostEstimate(
            flops=0, bytes_accessed=2 * TOK * D, transcendentals=0
        ),
        name="half",
    )(at, tokens)


def grad_kernel(blocks, mine, theirs, cot, cot_theirs, out, *rest):
    dims = (((0,), (0,)), ((), ()))
    total = lax.dot_general(mine[...], cot[...], dims, preferred_element_type=F32)
    total += lax.dot_general(
        theirs[...], cot_theirs[...], dims, preferred_element_type=F32
    )
    total = (total * SCALE).astype(out.dtype)

    @pl.when(pl.program_id(0) == 0)
    def _():
        out[...] = total

    for more in rest:

        @pl.when(pl.program_id(0) > 0)
        def _(more=more):
            more[0] = total


def grad_blocks(blocks, core, tokens, tokens_theirs, cot, cot_theirs):
    count = len(blocks)
    table = jnp.stack([2 * g + core for g in blocks] + blocks).astype(jnp.int32)
    whole = pl.BlockSpec((TOK, COLS), lambda m, b: (0, 0))
    return pl.pallas_call(
        grad_kernel,
        out_shape=[
            jax.ShapeDtypeStruct((512, COLS), BF),
            jax.ShapeDtypeStruct((count - 1, 512, COLS), BF),
        ][: min(count, 2)],
        grid_spec=pltpu.PrefetchScalarGridSpec(
            num_scalar_prefetch=1,
            grid=(count,),
            in_specs=[
                pl.BlockSpec((TOK, 512), lambda m, b: (0, b[m])),
                pl.BlockSpec((TOK, 512), lambda m, b: (0, b[count + m])),
                whole,
                whole,
            ],
            out_specs=[
                whole,
                pl.BlockSpec((1, 512, COLS), lambda m, b: (jnp.maximum(m - 1, 0), 0, 0)),
            ][: min(count, 2)],
        ),
        compiler_params=params(),
        cost_estimate=pl.CostEstimate(
            flops=count * 4 * TOK * 512 * COLS,
            bytes_accessed=(count * 2 + 2) << 20,
            transcendentals=0,
        ),
        name="grad",
    )(table, tokens, tokens_theirs, cot, cot_theirs)


def w_pieces(kind, at, sources, mine, dy):
    z, y, c = at[1], at[2], at[4]
    core = c if mine else 1 - c
    if kind == "x":
        (chunk, xs) = sources
        pieces = [(chunk.at[pl.ds(zh * 4, 4)], zh) for zh in range(2)]
        columns = []
        for zl, d in itertools.product(range(2), range(2)):
            f = zl * 8 + ((y + d) & 3) * 2 + core
            columns.append((f * 512 + xs * 128, (zl * 2 + d) * 128, 128))
    else:
        (chunks, zs) = sources
        pieces = [
            (chunk.at[pl.ds(0, 4), dy], zc >> 1) for chunk, zc in zip(chunks, zs)
        ]
        f = (zs[0] & 1) * 8 + ((y + 2 + dy) & 3) * 2 + core
        columns = [(f * 512, 0, 512)]
    return pieces, columns


def fold_kernel(steps, pairs, first, last, *refs):
    refs = list(refs)
    at, tokens, cot = refs[:3]
    refs = refs[3:]
    x_mine = [refs.pop(0) for _ in steps]
    x_theirs = [refs.pop(0) for _ in steps]
    z_mine = [[refs.pop(0) for _ in pair] for pair in pairs]
    z_theirs = [[refs.pop(0) for _ in pair] for pair in pairs]
    if not first:
        acc_in, _, _ = refs.pop(0), refs.pop(0), refs.pop(0)
    grad_out, weights_out, key_out = refs.pop(0), refs.pop(0), refs.pop(0)
    w, tok, grad, cot_v, acc, w_sem, tok_sem, out_sem, own_sem, cot_sem, acc_sem = (
        refs[:11]
    )
    if last:
        key_v = refs[11]
    x, z, y, c = at[0], at[1], at[2], at[4]
    way = 1 - 2 * c

    groups = []
    for s, mine, theirs in zip(steps, x_mine, x_theirs):
        groups.append(("x", (mine, ((x - way * s + 8) & 3)), True, 0))
        groups.append(("x", (theirs, ((x + way * s + 8) & 3)), False, 0))
    for pair, mine, theirs in zip(pairs, z_mine, z_theirs):
        zs_mine = [((z - way * s + 8) & 3) for s in pair]
        zs_theirs = [((z + way * s + 8) & 3) for s in pair]
        for dy in range(2):
            groups.append(("z", (mine, zs_mine), True, dy))
            groups.append(("z", (theirs, zs_theirs), False, dy))
    count = len(groups)

    def loads(i):
        kind, sources, is_mine, dy = groups[i]
        slot = i % 3
        pieces, columns = w_pieces(kind, at, sources, is_mine, dy)
        for src, zh in pieces:
            pltpu.make_async_copy(src, w.at[slot, :, zh], w_sem.at[slot]).start()
        for a, b, n in columns:
            pltpu.make_async_copy(
                tokens.at[:, pl.ds(pl.multiple_of(a, 128), n)],
                tok.at[slot, :, pl.ds(b, n)],
                tok_sem.at[slot],
            ).start()

    def weights_store(i):
        kind, sources, is_mine, dy = groups[i]
        slot = i % 3
        return pltpu.make_async_copy(
            w.at[slot, (z & 1) * 2], weights_out.at[sources[1]], own_sem.at[slot]
        )

    def stores(i):
        kind, sources, is_mine, dy = groups[i]
        slot = i % 3
        _, columns = w_pieces(kind, at, sources, is_mine, dy)
        for a, b, n in columns:
            pltpu.make_async_copy(
                grad.at[slot, :, pl.ds(b, n)],
                grad_out.at[:, pl.ds(pl.multiple_of(a, 128), n)],
                out_sem.at[slot],
            ).start()

    def whole(buffer, sem, slot):
        return pltpu.make_async_copy(buffer.at[slot], buffer.at[slot], sem.at[slot])

    cot_copy = pltpu.make_async_copy(cot, cot_v, cot_sem)
    cot_copy.start()
    loads(0)
    loads(1)
    if first:
        acc[...] = jnp.zeros_like(acc)
    else:
        acc_copy = pltpu.make_async_copy(acc_in, acc, acc_sem)
        acc_copy.start()
    cot_copy.wait()

    @pl.loop(0, count)
    def _(i):
        slot = lax.rem(i, 3)
        for k in range(2, count):

            @pl.when(i + 2 == k)
            def _(k=k):
                loads(k)

        whole(w, w_sem, slot).wait()
        for k in range(count):
            if groups[k][0] == "x" and groups[k][2]:

                @pl.when(i == k)
                def _(k=k):
                    weights_store(k).start()

        @pl.when(i >= 3)
        def _():
            whole(grad, out_sem, slot).wait()

        rows = w[slot].reshape(512, COLS)
        out = lax.dot_general(
            cot_v[...], rows, (((1,), (1,)), ((), ())), preferred_element_type=F32
        )
        grad[slot] = (out * SCALE).astype(BF)
        for k in range(count):

            @pl.when(i == k)
            def _(k=k):
                stores(k)

        whole(tok, tok_sem, slot).wait()
        if not first:

            @pl.when(i == 0)
            def _():
                acc_copy.wait()

        acc[...] += jnp.dot(tok[slot], rows, preferred_element_type=F32)
        for k in range(count):
            if groups[k][0] == "x" and groups[k][2]:

                @pl.when(i == k)
                def _(k=k):
                    weights_store(k).wait()

    if last:
        key_v[...] = (acc[...] * SCALE).astype(BF)
        key_copy = pltpu.make_async_copy(key_v, key_out, acc_sem)
    else:
        key_copy = pltpu.make_async_copy(acc, key_out, acc_sem)
    key_copy.start()
    for i in range(max(count - 3, 0), count):
        whole(grad, out_sem, i % 3).wait()
    key_copy.wait()


def fold(at, tokens, cot, steps, x_mine, x_theirs, pairs, z_mine, z_theirs, carry, last):
    first = carry is None
    operands = [at, tokens, cot, *x_mine, *x_theirs]
    operands += list(itertools.chain(*z_mine)) + list(itertools.chain(*z_theirs))
    aliases = {}
    if not first:
        operands += [carry[2]]
        aliases = {len(operands): 0, len(operands) + 1: 1}
        operands += carry[:2]
    shapes = [
        jax.ShapeDtypeStruct((TOK, D), BF),
        jax.ShapeDtypeStruct((4, 2, 64, COLS), BF),
        jax.ShapeDtypeStruct((TOK, COLS), BF if last else F32),
    ]
    dma = pltpu.SemaphoreType.DMA
    scratch = [
        pltpu.VMEM((3, 4, 2, 64, COLS), BF),
        pltpu.VMEM((3, TOK, 512), BF),
        pltpu.VMEM((3, TOK, 512), BF),
        pltpu.VMEM((TOK, COLS), BF),
        pltpu.VMEM((TOK, COLS), F32),
        dma((3,)),
        dma((3,)),
        dma((3,)),
        dma((3,)),
        dma(()),
        dma(()),
    ]
    if last:
        scratch += [pltpu.VMEM((TOK, COLS), BF)]
    groups = 2 * len(steps) + 4 * len(pairs)

    def kernel(*refs):
        fold_kernel(steps, pairs, first, last, *refs)

    return pl.pallas_call(
        kernel,
        out_shape=shapes,
        in_specs=[pl.BlockSpec(memory_space=pltpu.SMEM)] + [ANY] * (len(operands) - 1),
        out_specs=[ANY] * len(shapes),
        scratch_shapes=scratch,
        input_output_aliases=aliases,
        compiler_params=params(),
        cost_estimate=pl.CostEstimate(
            flops=groups * 4 * TOK * 512 * COLS,
            bytes_accessed=groups * (2 << 20) + (4 << 20),
            transcendentals=0,
        ),
        name="fold",
    )(*operands)


def per_device(deltas, outer_weights, momentum, tokens, key_cot):
    x, zh, zl, y, c = [lax.axis_index(a) for a in AXES]
    z = zh * 2 + zl
    way = 1 - 2 * c
    at = jnp.stack([x, z, y, zl, c]).astype(jnp.int32)
    blocks = deltas[0]

    own_at = x * 2 + zh
    summed = lax.dynamic_slice_in_dim(blocks, own_at * 64, 64, 0).astype(F32)
    for dx, dh in ((2, 1), (1, 1), (3, 1), (2, 0), (0, 1), (1, 0), (3, 0)):
        there = ((x + dx) & 3) * 2 + ((zh + dh) & 1)
        piece = lax.dynamic_slice_in_dim(blocks, there * 64, 64, 0)
        got = permute(
            piece, lambda px, pz, py, pc: (px + dx, pz + 2 * dh, py, pc)
        )
        summed = summed + got.astype(F32)
    mean_delta = summed / 8
    moment_next = MOMENTUM_RATE * momentum[0, 0] + mean_delta
    outer_next = outer_weights[0, 0] - OUTER_RATE * (
        mean_delta + MOMENTUM_RATE * moment_next
    )
    owned = outer_next.astype(BF)

    tokens_theirs = swap_core(other_half(at, tokens))
    cot_theirs = swap_core(key_cot)

    def grads(half, steps, tokens_theirs):
        zl_to = 1 - zl if half == 0 else zl
        blocks = [zl_to * 4 + ((y - way * (s + 1) + 8) & 3) for s in steps]
        return grad_blocks(blocks, c, tokens, tokens_theirs, key_cot, cot_theirs)

    def add(*parts):
        total = parts[0].astype(F32)
        for part in parts[1:]:
            total = total + part.astype(F32)
        return total

    (first,) = grads(0, (0,), tokens_theirs)
    owned, first, late = lax.optimization_barrier((owned, first, tokens_theirs))
    second, rest = grads(0, (1, 2, 3), late)

    def rows_from(value, dx=0, dz=0, dy=0):
        return permute(
            value, lambda px, pz, py, pc: (px - dx, pz - dz, py - dy, pc)
        )

    def in_order(parts, here):
        whole = jnp.zeros((4, *parts[0].shape), BF)
        for d, part in enumerate(parts):
            whole = lax.dynamic_update_slice_in_dim(
                whole, part[None], (here + d) & 3, 0
            )
        return whole

    by_y = [owned] + [rows_from(owned, dy=d) for d in (1, 2, 3)]
    a0 = jnp.stack(by_y[:2])
    b0 = jnp.stack(by_y[2:])
    a0, b0, rest, late = lax.optimization_barrier((a0, b0, rest, late))
    first_b, rest_b = grads(1, (0, 1, 2, 3), late)
    a1 = in_order([a0] + [rows_from(a0, dz=d) for d in (1, 2, 3)], z)
    b1 = in_order([b0] + [rows_from(b0, dx=d) for d in (1, 2, 3)], x)
    a1, b1, rest_b = lax.optimization_barrier((a1, b1, rest_b))
    a_mine, b_mine = [a1], [b1]
    a_theirs, b_theirs = [swap_core(a1)], [swap_core(b1)]

    def fold_of(steps, pairs, carry, last):
        return fold(
            at, tokens, key_cot, steps,
            [a_mine[s].reshape(8, 64, COLS) for s in steps],
            [a_theirs[s].reshape(8, 64, COLS) for s in steps],
            pairs,
            [[b_mine[s] for s in pair] for pair in pairs],
            [[b_theirs[s] for s in pair] for pair in pairs],
            carry, last,
        )

    carry = None
    for s, pairs in ((1, ()), (2, ()), (3, ((0, 2),))):
        a_next, b_next = ring_x(a_mine[-1]), ring_z(b_mine[-1])
        carry = fold_of((s - 1,), pairs, carry, False)
        if s < 3:
            a_next, b_next, *carry = lax.optimization_barrier((a_next, b_next, *carry))
        a_mine.append(a_next)
        b_mine.append(b_next)
        a_theirs.append(swap_core(a_next))
        b_theirs.append(swap_core(b_next))
    grad_tokens, shard_weights, keys_out = fold_of((3,), ((1, 3),), carry, True)
    shard_weights = shard_weights.reshape(512, COLS)

    arrived = ring_y(first)
    arrived = ring_y(add(second, arrived).astype(BF))
    arrived = ring_y(add(rest[0], arrived).astype(BF))
    crossed = add(rest[1], arrived).astype(BF)
    crossed = permute(crossed, lambda px, pz, py, pc: (px, pz ^ 1, py, pc))
    arrived = ring_y(first_b)
    arrived = ring_y(add(rest_b[0], arrived).astype(BF))
    arrived = ring_y(add(rest_b[1], arrived).astype(BF))
    grad_shard = add(rest_b[2], arrived, crossed)

    return (
        outer_next[None, None],
        moment_next[None, None],
        shard_weights,
        keys_out,
        grad_tokens,
        grad_shard[None],
    )


def solution(mesh):
    fine = Mesh(mesh.devices.reshape(SIZES), AXES)
    rep, fsdp = ("x", "zh"), ("zl", "y", "c")
    return jax.shard_map(
        per_device,
        mesh=fine,
        in_specs=(
            P(rep, fsdp, None),
            P(fsdp, rep, None, None),
            P(fsdp, rep, None, None),
            P(AXES, None),
            P(AXES, None),
        ),
        out_specs=(
            P(fsdp, rep, None, None),
            P(fsdp, rep, None, None),
            P(fsdp, None),
            P(AXES, None),
            P(AXES, None),
            P(rep, fsdp, None),
        ),
        check_vma=False,
    )
```

```python
import itertools

import jax
import jax.numpy as jnp
import numpy as np
from jax import lax
from jax.experimental import pallas as pl
from jax.experimental.pallas import tpu as pltpu
from jax.sharding import Mesh, PartitionSpec as P

MOMENTUM_RATE = 0.9
OUTER_RATE = 0.7
AXES = ("x", "zh", "zl", "y", "c")
SIZES = (4, 2, 2, 4, 2)
TOK = 512
D = 8192
COLS = 1024
SCALE = D ** (-0.5)
VMEM = 48 * 1024 * 1024
ANY = pl.BlockSpec(memory_space=pl.ANY)
BF = jnp.bfloat16
F32 = jnp.float32


def permute(value, to):
    pairs = []
    for x, zh, zl, y, c in itertools.product(*[range(n) for n in SIZES]):
        tx, tz, ty, tc = to(x, zh * 2 + zl, y, c)
        tz = tz % 4
        target = (tx % 4, tz // 2, tz % 2, ty % 4, tc % 2)
        pairs.append(
            (
                int(np.ravel_multi_index((x, zh, zl, y, c), SIZES)),
                int(np.ravel_multi_index(target, SIZES)),
            )
        )
    return lax.ppermute(value, AXES, pairs)


def swap_core(value):
    return permute(value, lambda x, z, y, c: (x, z, y, 1 - c))


def ring_y(value):
    return permute(value, lambda x, z, y, c: (x, z, y + 1 - 2 * c, c))


def params(**more):
    return pltpu.CompilerParams(vmem_limit_bytes=VMEM, **more)


def half_kernel(at, tokens, out, held, in_sem, out_sem):
    c = at[4]
    loads = [
        pltpu.make_async_copy(
            tokens.at[:, pl.ds(pl.multiple_of((2 * g + 1 - c) * 512, 512), 512)],
            held.at[:, pl.ds(g * 512, 512)],
            in_sem.at[g],
        )
        for g in range(8)
    ]
    stores = [
        pltpu.make_async_copy(
            held.at[:, pl.ds(g * 512, 512)],
            out.at[:, pl.ds(g * 512, 512)],
            out_sem.at[g],
        )
        for g in range(8)
    ]
    for load in loads:
        load.start()
    for load, store in zip(loads, stores):
        load.wait()
        store.start()
    for store in stores:
        store.wait()


def other_half(at, tokens):
    return pl.pallas_call(
        half_kernel,
        out_shape=jax.ShapeDtypeStruct((TOK, D // 2), BF),
        in_specs=[pl.BlockSpec(memory_space=pltpu.SMEM), ANY],
        out_specs=ANY,
        scratch_shapes=[
            pltpu.VMEM((TOK, D // 2), BF),
            pltpu.SemaphoreType.DMA((8,)),
            pltpu.SemaphoreType.DMA((8,)),
        ],
        compiler_params=params(),
        cost_estimate=pl.CostEstimate(
            flops=0, bytes_accessed=2 * TOK * D, transcendentals=0
        ),
        name="half",
    )(at, tokens)


def grad_kernel(blocks, mine, theirs, cot, cot_theirs, out, *rest):
    dims = (((0,), (0,)), ((), ()))
    total = lax.dot_general(mine[...], cot[...], dims, preferred_element_type=F32)
    total += lax.dot_general(
        theirs[...], cot_theirs[...], dims, preferred_element_type=F32
    )
    total = (total * SCALE).astype(out.dtype)

    @pl.when(pl.program_id(0) == 0)
    def _():
        out[...] = total

    for more in rest:

        @pl.when(pl.program_id(0) > 0)
        def _(more=more):
            more[0] = total


def grad_blocks(blocks, core, tokens, tokens_theirs, cot, cot_theirs):
    count = len(blocks)
    table = jnp.stack([2 * g + core for g in blocks] + blocks).astype(jnp.int32)
    whole = pl.BlockSpec((TOK, COLS), lambda m, b: (0, 0))
    return pl.pallas_call(
        grad_kernel,
        out_shape=[
            jax.ShapeDtypeStruct((512, COLS), BF),
            jax.ShapeDtypeStruct((count - 1, 512, COLS), BF),
        ][: min(count, 2)],
        grid_spec=pltpu.PrefetchScalarGridSpec(
            num_scalar_prefetch=1,
            grid=(count,),
            in_specs=[
                pl.BlockSpec((TOK, 512), lambda m, b: (0, b[m])),
                pl.BlockSpec((TOK, 512), lambda m, b: (0, b[count + m])),
                whole,
                whole,
            ],
            out_specs=[
                whole,
                pl.BlockSpec((1, 512, COLS), lambda m, b: (jnp.maximum(m - 1, 0), 0, 0)),
            ][: min(count, 2)],
        ),
        compiler_params=params(),
        cost_estimate=pl.CostEstimate(
            flops=0,
            bytes_accessed=1 << 20,
            transcendentals=0,
        ),
        name="grad",
    )(table, tokens, tokens_theirs, cot, cot_theirs)


OFFSETS = (0, -1, 2, 1)


def fold_kernel(groups, chunks, first, last, *refs):
    refs = list(refs)
    at, tokens, cot = refs[:3]
    refs = refs[3:]
    mine = {key: refs.pop(0) for key in chunks}
    theirs = {key: refs.pop(0) for key in chunks}
    if not first:
        acc_in, _, _ = refs.pop(0), refs.pop(0), refs.pop(0)
    grad_out, weights_out, key_out = refs.pop(0), refs.pop(0), refs.pop(0)
    w, tok, grad, cot_v, acc, w_sem, tok_sem, out_sem, own_sem, cot_sem, acc_sem = (
        refs[:11]
    )
    if last:
        key_v = refs[11]
    x, z, y, c = at[0], at[1], at[2], at[4]

    def part(held, s, dy):
        return held[s, dy] if (s, dy) in held else held[s].at[dy]

    def x_of(s):
        return (x + OFFSETS[s] + 4) & 3

    def z_of(s):
        return (z + OFFSETS[s] + 4) & 3

    def columns_of(group):
        if group[0] == "x":
            _, s, dy = group
            return [
                (
                    (zl * 8 + ((y + dy) & 3) * 2 + p) * 512 + x_of(s) * 128,
                    (zl * 2 + p) * 128,
                    128,
                )
                for zl in range(2)
                for p in range(2)
            ]
        _, (s, t), dy, p = group
        return [(((z_of(s) & 1) * 8 + ((y + 2 + dy) & 3) * 2 + p) * 512, 0, 512)]

    def load_weights(group, slot):
        def start(held):
            if group[0] == "x":
                _, s, dy = group
                for zl, zh in itertools.product(range(2), range(2)):
                    pltpu.make_async_copy(
                        part(held, s, dy).at[zh * 2 + zl],
                        w.at[slot, pl.ds(zl * 2, 2), zh],
                        w_sem.at[slot],
                    ).start()
            else:
                _, pair, dy, p = group
                for s in pair:
                    pltpu.make_async_copy(
                        part(held, s, dy).at[:, p],
                        w.at[slot, :, z_of(s) >> 1],
                        w_sem.at[slot],
                    ).start()

        here = 0 if group[0] == "x" else 1

        @pl.when(c == here)
        def _():
            start(mine)

        @pl.when(c != here)
        def _():
            start(theirs)

    count = len(groups)

    def loads(i):
        slot = i % 3
        load_weights(groups[i], slot)
        for a, b, n in columns_of(groups[i]):
            pltpu.make_async_copy(
                tokens.at[:, pl.ds(pl.multiple_of(a, 128), n)],
                tok.at[slot, :, pl.ds(b, n)],
                tok_sem.at[slot],
            ).start()

    def holds_own(group):
        return group[0] == "x" and group[2] == 0

    def weights_store(i):
        slot = i % 3
        return pltpu.make_async_copy(
            w.at[slot, (z & 1) * 2 + c],
            weights_out.at[x_of(groups[i][1])],
            own_sem.at[slot],
        )

    def stores(i):
        slot = i % 3
        for a, b, n in columns_of(groups[i]):
            pltpu.make_async_copy(
                grad.at[slot, :, pl.ds(b, n)],
                grad_out.at[:, pl.ds(pl.multiple_of(a, 128), n)],
                out_sem.at[slot],
            ).start()

    def whole(buffer, sem, slot):
        return pltpu.make_async_copy(buffer.at[slot], buffer.at[slot], sem.at[slot])

    cot_copy = pltpu.make_async_copy(cot, cot_v, cot_sem)
    cot_copy.start()
    loads(0)
    loads(1)
    if first:
        acc[...] = jnp.zeros_like(acc)
    else:
        acc_copy = pltpu.make_async_copy(acc_in, acc, acc_sem)
        acc_copy.start()
    cot_copy.wait()

    @pl.loop(0, count)
    def _(i):
        slot = lax.rem(i, 3)
        for k in range(2, count):

            @pl.when(i + 2 == k)
            def _(k=k):
                loads(k)

        whole(w, w_sem, slot).wait()
        for k in range(count):
            if holds_own(groups[k]):

                @pl.when(i == k)
                def _(k=k):
                    weights_store(k).start()

        @pl.when(i >= 3)
        def _():
            whole(grad, out_sem, slot).wait()

        rows = w[slot].reshape(512, COLS)
        out = lax.dot_general(
            cot_v[...], rows, (((1,), (1,)), ((), ())), preferred_element_type=F32
        )
        grad[slot] = (out * SCALE).astype(BF)
        for k in range(count):

            @pl.when(i == k)
            def _(k=k):
                stores(k)

        whole(tok, tok_sem, slot).wait()
        if not first:

            @pl.when(i == 0)
            def _():
                acc_copy.wait()

        acc[...] += jnp.dot(tok[slot], rows, preferred_element_type=F32)
        for k in range(count):
            if holds_own(groups[k]):

                @pl.when(i == k)
                def _(k=k):
                    weights_store(k).wait()

    if last:
        key_v[...] = (acc[...] * SCALE).astype(BF)
        key_copy = pltpu.make_async_copy(key_v, key_out, acc_sem)
    else:
        key_copy = pltpu.make_async_copy(acc, key_out, acc_sem)
    key_copy.start()
    for i in range(max(count - 3, 0), count):
        whole(grad, out_sem, i % 3).wait()
    key_copy.wait()


def fold(at, tokens, cot, groups, mine, theirs, carry, last):
    first = carry is None
    operands = [at, tokens, cot, *mine.values(), *theirs.values()]
    aliases = {}
    if not first:
        operands += [carry[2]]
        aliases = {len(operands): 0, len(operands) + 1: 1}
        operands += carry[:2]
    shapes = [
        jax.ShapeDtypeStruct((TOK, D), BF),
        jax.ShapeDtypeStruct((4, 2, 64, COLS), BF),
        jax.ShapeDtypeStruct((TOK, COLS), BF if last else F32),
    ]
    dma = pltpu.SemaphoreType.DMA
    scratch = [
        pltpu.VMEM((3, 4, 2, 64, COLS), BF),
        pltpu.VMEM((3, TOK, 512), BF),
        pltpu.VMEM((3, TOK, 512), BF),
        pltpu.VMEM((TOK, COLS), BF),
        pltpu.VMEM((TOK, COLS), F32),
        dma((3,)),
        dma((3,)),
        dma((3,)),
        dma((3,)),
        dma(()),
        dma(()),
    ]
    if last:
        scratch += [pltpu.VMEM((TOK, COLS), BF)]
    def kernel(*refs):
        fold_kernel(groups, list(mine), first, last, *refs)

    return pl.pallas_call(
        kernel,
        out_shape=shapes,
        in_specs=[pl.BlockSpec(memory_space=pltpu.SMEM)] + [ANY] * (len(operands) - 1),
        out_specs=[ANY] * len(shapes),
        scratch_shapes=scratch,
        input_output_aliases=aliases,
        compiler_params=params(),
        cost_estimate=pl.CostEstimate(
            flops=0, bytes_accessed=1 << 20,
            transcendentals=0,
        ),
        name="fold",
    )(*operands)


def per_device(deltas, outer_weights, momentum, tokens, key_cot):
    x, zh, zl, y, c = [lax.axis_index(a) for a in AXES]
    z = zh * 2 + zl
    way = 1 - 2 * c
    at = jnp.stack([x, z, y, zl, c]).astype(jnp.int32)
    blocks = deltas[0]

    tokens_theirs = swap_core(other_half(at, tokens))
    cot_theirs = swap_core(key_cot)

    def grads(which, tokens_theirs):
        blocks = [
            (zl if half else 1 - zl) * 4 + ((y - way * (s + 1) + 8) & 3)
            for half, s in which
        ]
        return grad_blocks(blocks, c, tokens, tokens_theirs, key_cot, cot_theirs)

    def add(*parts):
        total = parts[0].astype(F32)
        for part in parts[1:]:
            total = total + part.astype(F32)
        return total

    by_x = blocks.reshape(4, 2, 64, COLS)
    got = []
    for d in (2, 1, 3):
        piece = lax.dynamic_index_in_dim(by_x, (x + d) & 3, 0, False)
        got.append(permute(piece, lambda px, pz, py, pc: (px + d, pz, py, pc)))
    first, first_b = grads([(0, 0), (1, 0)], tokens_theirs)
    *got, first, first_b = lax.optimization_barrier((*got, first, first_b[0]))
    arrived, arrived_b = ring_y(first), ring_y(first_b)
    part = add(lax.dynamic_index_in_dim(by_x, x, 0, False), *got)
    crossing = lax.dynamic_index_in_dim(part, 1 - zh, 0, False).astype(BF)
    crossing = permute(crossing, lambda px, pz, py, pc: (px, pz + 2, py, pc))
    summed = add(lax.dynamic_index_in_dim(part, zh, 0, False), crossing)
    mean_delta = summed / 8
    moment_next = MOMENTUM_RATE * momentum[0, 0] + mean_delta
    outer_next = outer_weights[0, 0] - OUTER_RATE * (
        mean_delta + MOMENTUM_RATE * moment_next
    )
    owned = outer_next.astype(BF)

    def short_way(value, d):
        return permute(
            value,
            lambda px, pz, py, pc: (px - d * pc, pz - d * (1 - pc), py, pc),
        )

    def long_way(value, d):
        return permute(
            value,
            lambda px, pz, py, pc: (px + d * (1 - pc), pz + d * pc, py, pc),
        )

    def in_order(parts, here):
        whole = jnp.zeros((2, 4, 2, 64, COLS), BF)
        for d, part in enumerate(parts):
            whole = lax.dynamic_update_slice_in_dim(
                whole, part[:, None], (here + d) & 3, 1
            )
        return whole

    owned, late = lax.optimization_barrier((owned, tokens_theirs))
    second, second_b = grads([(0, 1), (1, 1)], late)
    other, arrived = lax.optimization_barrier((swap_core(owned), arrived))
    both = jnp.where(c == 0, jnp.stack([owned, other]), jnp.stack([other, owned]))
    near = permute(both, lambda px, pz, py, pc: (px, pz, py - 1 + 2 * pc, pc))
    far = permute(both, lambda px, pz, py, pc: (px, pz, py + 2 * pc, pc))
    c0 = jnp.stack([far, near])
    c0, second, second_b, late = lax.optimization_barrier(
        (c0, second, second_b[0], late)
    )
    third, rest = grads([(0, 2), (0, 3), (1, 2), (1, 3)], late)
    parts = [short_way(c0, d) for d in (1, 2, 3)]
    arrived = ring_y(add(second, arrived).astype(BF))
    parts[0], arrived_b = lax.optimization_barrier((parts[0], arrived_b))
    c1 = in_order([c0] + parts, jnp.where(c == 0, z, x))
    c1, third, rest, arrived = lax.optimization_barrier((c1, third, rest, arrived))

    mine, theirs = {0: c1}, {0: swap_core(c1)}
    mine[1], mine[3] = long_way(c1, 1), long_way(c1, -1)

    def fold_of(groups, keys, carry, last):
        return fold(
            at, tokens, key_cot, groups,
            {k: mine[k] for k in keys}, {k: theirs[k] for k in keys}, carry, last,
        )

    carry = fold_of([("x", 0, 0), ("x", 0, 1)], [0], None, False)
    arrived = ring_y(add(third, arrived).astype(BF))
    mine[1], mine[3], arrived, arrived_b, *carry = lax.optimization_barrier(
        (mine[1], mine[3], arrived, arrived_b, *carry)
    )
    mine[2, 0] = long_way(mine[1][0], 1)
    mine[2, 1] = long_way(mine[3][1], -1)
    theirs[1], theirs[3] = swap_core(mine[1]), swap_core(mine[3])
    crossed = add(rest[0], arrived).astype(BF)
    crossed = [
        permute(half, lambda px, pz, py, pc: (px, pz ^ 1, py, pc))
        for half in (crossed[:256], crossed[256:])
    ]
    arrived_b = ring_y(add(second_b, arrived_b).astype(BF))
    carry = fold_of(
        [("x", s, dy) for s in (1, 3) for dy in range(2)]
        + [("z", (1, 3), dy, p) for dy in range(2) for p in range(2)],
        [1, 3], carry, False,
    )
    mine[2, 0], mine[2, 1], arrived_b, crossed[0], *carry = lax.optimization_barrier(
        (mine[2, 0], mine[2, 1], arrived_b, crossed[0], *carry)
    )
    theirs[2, 0], theirs[2, 1] = swap_core(mine[2, 0]), swap_core(mine[2, 1])
    arrived_b = ring_y(add(rest[1], arrived_b).astype(BF))
    grad_tokens, shard_weights, keys_out = fold_of(
        [("x", 2, dy) for dy in range(2)]
        + [("z", (0, 2), dy, p) for dy in range(2) for p in range(2)],
        [0, (2, 0), (2, 1)], carry, True,
    )
    arrived_b, *crossed, keys_out = lax.optimization_barrier(
        (arrived_b, *crossed, keys_out)
    )
    grad_shard = add(rest[2], arrived_b, jnp.concatenate(crossed))
    shard_weights = shard_weights.reshape(512, COLS)

    return (
        outer_next[None, None],
        moment_next[None, None],
        shard_weights,
        keys_out,
        grad_tokens,
        grad_shard[None],
    )


def solution(mesh):
    fine = Mesh(mesh.devices.reshape(SIZES), AXES)
    rep, fsdp = ("x", "zh"), ("zl", "y", "c")
    return jax.shard_map(
        per_device,
        mesh=fine,
        in_specs=(
            P(rep, fsdp, None),
            P(fsdp, rep, None, None),
            P(fsdp, rep, None, None),
            P(AXES, None),
            P(AXES, None),
        ),
        out_specs=(
            P(fsdp, rep, None, None),
            P(fsdp, rep, None, None),
            P(fsdp, None),
            P(AXES, None),
            P(AXES, None),
            P(rep, fsdp, None),
        ),
        check_vma=False,
    )
```

```python
import functools
import itertools

import jax
import jax.numpy as jnp
import numpy as np
from jax import lax
from jax.experimental import pallas as pl
from jax.experimental.pallas import tpu as pltpu
from jax.sharding import Mesh, PartitionSpec as P

MOMENTUM_RATE = 0.9
OUTER_RATE = 0.7
AXES = ("x", "zh", "zl", "y", "c")
SIZES = (4, 2, 2, 4, 2)
TOK = 512
D = 8192
COLS = 1024
SCALE = D ** (-0.5)
VMEM = 48 * 1024 * 1024
ANY = pl.BlockSpec(memory_space=pl.ANY)
BF = jnp.bfloat16
F32 = jnp.float32


def permute(value, to):
    pairs = []
    for x, zh, zl, y, c in itertools.product(*[range(n) for n in SIZES]):
        tx, tz, ty, tc = to(x, zh * 2 + zl, y, c)
        tz = tz % 4
        target = (tx % 4, tz // 2, tz % 2, ty % 4, tc % 2)
        pairs.append(
            (
                int(np.ravel_multi_index((x, zh, zl, y, c), SIZES)),
                int(np.ravel_multi_index(target, SIZES)),
            )
        )
    return lax.ppermute(value, AXES, pairs)


def swap_core(value):
    return permute(value, lambda x, z, y, c: (x, z, y, 1 - c))


def ring_y(value):
    return permute(value, lambda x, z, y, c: (x, z, y + 1 - 2 * c, c))


def params(**more):
    return pltpu.CompilerParams(vmem_limit_bytes=VMEM, **more)


def half_kernel(at, tokens, out, held, in_sem, out_sem):
    c = at[4]
    loads = [
        pltpu.make_async_copy(
            tokens.at[:, pl.ds(pl.multiple_of((2 * g + 1 - c) * 512, 512), 512)],
            held.at[:, pl.ds(g * 512, 512)],
            in_sem.at[g],
        )
        for g in range(8)
    ]
    stores = [
        pltpu.make_async_copy(
            held.at[:, pl.ds(g * 512, 512)],
            out.at[:, pl.ds(g * 512, 512)],
            out_sem.at[g],
        )
        for g in range(8)
    ]
    for load in loads:
        load.start()
    for load, store in zip(loads, stores):
        load.wait()
        store.start()
    for store in stores:
        store.wait()


def other_half(at, tokens):
    return pl.pallas_call(
        half_kernel,
        out_shape=jax.ShapeDtypeStruct((TOK, D // 2), BF),
        in_specs=[pl.BlockSpec(memory_space=pltpu.SMEM), ANY],
        out_specs=ANY,
        scratch_shapes=[
            pltpu.VMEM((TOK, D // 2), BF),
            pltpu.SemaphoreType.DMA((8,)),
            pltpu.SemaphoreType.DMA((8,)),
        ],
        compiler_params=params(),
        cost_estimate=pl.CostEstimate(
            flops=0, bytes_accessed=2 * TOK * D, transcendentals=0
        ),
        name="half",
    )(at, tokens)


def grad_kernel(adds, blocks, mine, theirs, cot, cot_theirs, *refs):
    arrived, (out, *rest) = refs[:adds], refs[adds:]
    dims = (((0,), (0,)), ((), ()))
    total = lax.dot_general(mine[...], cot[...], dims, preferred_element_type=F32)
    total += lax.dot_general(
        theirs[...], cot_theirs[...], dims, preferred_element_type=F32
    )
    total = total * SCALE

    @pl.when(pl.program_id(0) == 0)
    def _():
        first = total
        for part in arrived:
            first = first + part[...].astype(F32)
        out[...] = first.astype(BF)

    for more in rest:

        @pl.when(pl.program_id(0) > 0)
        def _(more=more):
            more[0] = total.astype(BF)


def grad_blocks(blocks, core, tokens, tokens_theirs, cot, cot_theirs, arrived):
    count = len(blocks)
    table = jnp.stack([2 * g + core for g in blocks] + blocks).astype(jnp.int32)
    whole = pl.BlockSpec((TOK, COLS), lambda m, b: (0, 0))
    return pl.pallas_call(
        functools.partial(grad_kernel, len(arrived)),
        out_shape=[
            jax.ShapeDtypeStruct((512, COLS), BF),
            jax.ShapeDtypeStruct((count - 1, 512, COLS), BF),
        ][: min(count, 2)],
        grid_spec=pltpu.PrefetchScalarGridSpec(
            num_scalar_prefetch=1,
            grid=(count,),
            in_specs=[
                pl.BlockSpec((TOK, 512), lambda m, b: (0, b[m])),
                pl.BlockSpec((TOK, 512), lambda m, b: (0, b[count + m])),
                whole,
                whole,
            ]
            + [whole] * len(arrived),
            out_specs=[
                whole,
                pl.BlockSpec((1, 512, COLS), lambda m, b: (jnp.maximum(m - 1, 0), 0, 0)),
            ][: min(count, 2)],
        ),
        compiler_params=params(),
        cost_estimate=pl.CostEstimate(
            flops=count * 4 * TOK * 512 * COLS,
            bytes_accessed=(count * 2 + 2) << 20,
            transcendentals=0,
        ),
        name="grad",
    )(table, tokens, tokens_theirs, cot, cot_theirs, *arrived)


OFFSETS = (0, -1, 2, 1)


def fold_kernel(groups, mine, theirs, first, last, *refs):
    refs = list(refs)
    at, tokens, cot = refs[:3]
    refs = refs[3:]
    mine = {key: refs.pop(0) for key in mine}
    theirs = {key: refs.pop(0) for key in theirs}
    if not first:
        acc_in, _, _ = refs.pop(0), refs.pop(0), refs.pop(0)
    grad_out, weights_out, key_out = refs.pop(0), refs.pop(0), refs.pop(0)
    w, tok, grad, cot_v, acc, w_sem, tok_sem, out_sem, own_sem, cot_sem, acc_sem = (
        refs[:11]
    )
    if last:
        key_v = refs[11]
    x, z, y, c = at[0], at[1], at[2], at[4]

    def part(held, s, dy):
        return held[s, dy] if (s, dy) in held else held[s].at[dy]

    def x_of(s):
        return (x + OFFSETS[s] + 4) & 3

    def z_of(s):
        return (z + OFFSETS[s] + 4) & 3

    def columns_of(group):
        if group[0] == "x":
            _, s, dy = group
            return [
                (
                    (zl * 8 + ((y + dy) & 3) * 2 + p) * 512 + x_of(s) * 128,
                    (zl * 2 + p) * 128,
                    128,
                )
                for zl in range(2)
                for p in range(2)
            ]
        _, (s, t), dy, p = group
        return [(((z_of(s) & 1) * 8 + ((y + 2 + dy) & 3) * 2 + p) * 512, 0, 512)]

    def each(i, do):
        if groups[i][0] == groups[i][1]:
            do(groups[i][0], None)
            return
        for core, group in enumerate(groups[i]):

            @pl.when(c == core)
            def _(group=group, core=core):
                do(group, core)

    def load_weights(group, slot, core):
        def start(held):
            if group[0] == "x":
                _, s, dy = group
                for zl, zh in itertools.product(range(2), range(2)):
                    pltpu.make_async_copy(
                        part(held, s, dy).at[zh * 2 + zl],
                        w.at[slot, pl.ds(zl * 2, 2), zh],
                        w_sem.at[slot],
                    ).start()
            else:
                _, pair, dy, p = group
                for s in pair:
                    pltpu.make_async_copy(
                        part(held, s, dy).at[:, p],
                        w.at[slot, :, z_of(s) >> 1],
                        w_sem.at[slot],
                    ).start()

        here = 0 if group[0] == "x" else 1
        if core is not None:
            start(mine if core == here else theirs)
            return

        @pl.when(c == here)
        def _():
            start(mine)

        @pl.when(c != here)
        def _():
            start(theirs)

    count = len(groups)

    def loads(i):
        slot = i % 3

        def start(group, core):
            load_weights(group, slot, core)
            for a, b, n in columns_of(group):
                pltpu.make_async_copy(
                    tokens.at[:, pl.ds(pl.multiple_of(a, 128), n)],
                    tok.at[slot, :, pl.ds(b, n)],
                    tok_sem.at[slot],
                ).start()

        each(i, start)

    def holds_own(group):
        return group[0] == "x" and group[2] == 0

    def weights_store(i, do):
        slot = i % 3

        def copy(group, core):
            if holds_own(group):
                do(
                    pltpu.make_async_copy(
                        w.at[slot, (z & 1) * 2 + c],
                        weights_out.at[x_of(group[1])],
                        own_sem.at[slot],
                    )
                )

        each(i, copy)

    def stores(i):
        slot = i % 3

        def start(group, core):
            for a, b, n in columns_of(group):
                pltpu.make_async_copy(
                    grad.at[slot, :, pl.ds(b, n)],
                    grad_out.at[:, pl.ds(pl.multiple_of(a, 128), n)],
                    out_sem.at[slot],
                ).start()

        each(i, start)

    def whole(buffer, sem, slot):
        return pltpu.make_async_copy(buffer.at[slot], buffer.at[slot], sem.at[slot])

    cot_copy = pltpu.make_async_copy(cot, cot_v, cot_sem)
    cot_copy.start()
    loads(0)
    loads(1)
    if first:
        acc[...] = jnp.zeros_like(acc)
    else:
        acc_copy = pltpu.make_async_copy(acc_in, acc, acc_sem)
        acc_copy.start()
    cot_copy.wait()

    @pl.loop(0, count)
    def _(i):
        slot = lax.rem(i, 3)
        for k in range(2, count):

            @pl.when(i + 2 == k)
            def _(k=k):
                loads(k)

        whole(w, w_sem, slot).wait()
        for k in range(count):
            if any(map(holds_own, groups[k])):

                @pl.when(i == k)
                def _(k=k):
                    weights_store(k, lambda copy: copy.start())

        @pl.when(i >= 3)
        def _():
            whole(grad, out_sem, slot).wait()

        rows = w[slot].reshape(512, COLS)
        out = lax.dot_general(
            cot_v[...], rows, (((1,), (1,)), ((), ())), preferred_element_type=F32
        )
        grad[slot] = (out * SCALE).astype(BF)
        for k in range(count):

            @pl.when(i == k)
            def _(k=k):
                stores(k)

        whole(tok, tok_sem, slot).wait()
        if not first:

            @pl.when(i == 0)
            def _():
                acc_copy.wait()

        acc[...] += jnp.dot(tok[slot], rows, preferred_element_type=F32)
        for k in range(count):
            if any(map(holds_own, groups[k])):

                @pl.when(i == k)
                def _(k=k):
                    weights_store(k, lambda copy: copy.wait())

    if last:
        key_v[...] = (acc[...] * SCALE).astype(BF)
        key_copy = pltpu.make_async_copy(key_v, key_out, acc_sem)
    else:
        key_copy = pltpu.make_async_copy(acc, key_out, acc_sem)
    key_copy.start()
    for i in range(max(count - 3, 0), count):
        whole(grad, out_sem, i % 3).wait()
    key_copy.wait()


def fold(at, tokens, cot, groups, mine, theirs, carry, last):
    first = carry is None
    operands = [at, tokens, cot, *mine.values(), *theirs.values()]
    aliases = {}
    if not first:
        operands += [carry[2]]
        aliases = {len(operands): 0, len(operands) + 1: 1}
        operands += carry[:2]
    shapes = [
        jax.ShapeDtypeStruct((TOK, D), BF),
        jax.ShapeDtypeStruct((4, 2, 64, COLS), BF),
        jax.ShapeDtypeStruct((TOK, COLS), BF if last else F32),
    ]
    dma = pltpu.SemaphoreType.DMA
    scratch = [
        pltpu.VMEM((3, 4, 2, 64, COLS), BF),
        pltpu.VMEM((3, TOK, 512), BF),
        pltpu.VMEM((3, TOK, 512), BF),
        pltpu.VMEM((TOK, COLS), BF),
        pltpu.VMEM((TOK, COLS), F32),
        dma((3,)),
        dma((3,)),
        dma((3,)),
        dma((3,)),
        dma(()),
        dma(()),
    ]
    if last:
        scratch += [pltpu.VMEM((TOK, COLS), BF)]
    def kernel(*refs):
        fold_kernel(groups, list(mine), list(theirs), first, last, *refs)

    return pl.pallas_call(
        kernel,
        out_shape=shapes,
        in_specs=[pl.BlockSpec(memory_space=pltpu.SMEM)] + [ANY] * (len(operands) - 1),
        out_specs=[ANY] * len(shapes),
        scratch_shapes=scratch,
        input_output_aliases=aliases,
        compiler_params=params(),
        cost_estimate=pl.CostEstimate(
            flops=0, bytes_accessed=1 << 20,
            transcendentals=0,
        ),
        name="fold",
    )(*operands)


def per_device(deltas, outer_weights, momentum, tokens, key_cot):
    x, zh, zl, y, c = [lax.axis_index(a) for a in AXES]
    z = zh * 2 + zl
    way = 1 - 2 * c
    at = jnp.stack([x, z, y, zl, c]).astype(jnp.int32)
    blocks = deltas[0]

    tokens_theirs = swap_core(other_half(at, tokens))
    cot_theirs = swap_core(key_cot)

    def grads(which, tokens_theirs, *arrived):
        blocks = [
            (zl if half else 1 - zl) * 4 + ((y - way * (s + 1) + 8) & 3)
            for half, s in which
        ]
        return grad_blocks(
            blocks, c, tokens, tokens_theirs, key_cot, cot_theirs, arrived
        )

    def add(*parts):
        total = parts[0].astype(F32)
        for part in parts[1:]:
            total = total + part.astype(F32)
        return total

    by_x = blocks.reshape(4, 2, 64, COLS)
    got = []
    for d in (2, 1, 3):
        piece = lax.dynamic_index_in_dim(by_x, (x + d) & 3, 0, False)
        got.append(permute(piece, lambda px, pz, py, pc: (px + d, pz, py, pc)))
    first, first_b = grads([(0, 0), (1, 0)], tokens_theirs)
    *got, first, first_b = lax.optimization_barrier((*got, first, first_b[0]))
    arrived, arrived_b = ring_y(first), ring_y(first_b)
    part = add(lax.dynamic_index_in_dim(by_x, x, 0, False), *got)
    crossing = lax.dynamic_index_in_dim(part, 1 - zh, 0, False).astype(BF)
    crossing = permute(crossing, lambda px, pz, py, pc: (px, pz + 2, py, pc))
    summed = add(lax.dynamic_index_in_dim(part, zh, 0, False), crossing)
    mean_delta = summed / 8
    moment_next = MOMENTUM_RATE * momentum[0, 0] + mean_delta
    outer_next = outer_weights[0, 0] - OUTER_RATE * (
        mean_delta + MOMENTUM_RATE * moment_next
    )
    owned = outer_next.astype(BF)

    def short_way(value, d):
        return permute(
            value,
            lambda px, pz, py, pc: (px - d * pc, pz - d * (1 - pc), py, pc),
        )

    def long_way(value, d):
        return permute(
            value,
            lambda px, pz, py, pc: (px + d * (1 - pc), pz + d * pc, py, pc),
        )

    def in_order(parts, here):
        whole = jnp.zeros((2, 4, 2, 64, COLS), BF)
        for d, part in enumerate(parts):
            whole = lax.dynamic_update_slice_in_dim(
                whole, part[:, None], (here + d) & 3, 1
            )
        return whole

    other = swap_core(owned)
    both = jnp.where(c == 0, jnp.stack([owned, other]), jnp.stack([other, owned]))
    near = permute(both, lambda px, pz, py, pc: (px, pz, py - 1 + 2 * pc, pc))
    far = permute(both, lambda px, pz, py, pc: (px, pz, py + 2 * pc, pc))
    c0 = jnp.stack([far, near])
    c0, late = lax.optimization_barrier((c0, tokens_theirs))
    second, second_b = grads([(0, 1), (1, 1)], late, arrived)
    parts = [short_way(c0, d) for d in (1, 2, 3)]
    arrived = ring_y(second)
    parts[0], arrived_b = lax.optimization_barrier((parts[0], arrived_b))
    second_b = second_b[0]
    c1 = in_order([c0] + parts, jnp.where(c == 0, z, x))
    c1, late = lax.optimization_barrier((c1, late))
    third, rest = grads([(0, 2), (0, 3), (1, 2), (1, 3)], late, arrived)

    mine, theirs = {0: c1}, {0: swap_core(c1)}
    mine[1], mine[3] = long_way(c1, 1), long_way(c1, -1)

    def fold_of(groups, keys, keys_theirs, carry, last):
        return fold(
            at, tokens, key_cot, groups,
            {k: mine[k] for k in keys}, {k: theirs[k] for k in keys_theirs}, carry, last,
        )

    own = [("x", 0, 0), ("x", 0, 1)]
    carry = fold_of(list(zip(own, own)), [0], [0], None, False)
    arrived = ring_y(third)
    mine[1], mine[3], arrived, arrived_b, *carry = lax.optimization_barrier(
        (mine[1], mine[3], arrived, arrived_b, *carry)
    )
    mine[2, 0] = long_way(mine[1][0], 1)
    mine[2, 1] = long_way(mine[3][1], -1)
    theirs[1], theirs[3] = swap_core(mine[1]), swap_core(mine[3])
    crossed = add(rest[0], arrived).astype(BF)
    crossed = [
        permute(half, lambda px, pz, py, pc: (px, pz ^ 1, py, pc))
        for half in (crossed[:192], crossed[192:])
    ]
    arrived_b = ring_y(add(second_b, arrived_b).astype(BF))
    near_a = [("x", s, dy) for s in (1, 3) for dy in range(2)]
    near_b = [("z", (1, 3), dy, p) for dy in range(2) for p in range(2)]
    carry = fold_of(list(zip(near_a, near_b)), [1, 3], [], carry, False)
    carry = fold_of(list(zip(near_b, near_a)), [], [1, 3], carry, False)
    mine[2, 0], mine[2, 1], arrived_b, crossed[0], *carry = lax.optimization_barrier(
        (mine[2, 0], mine[2, 1], arrived_b, crossed[0], *carry)
    )
    theirs[2, 0], theirs[2, 1] = swap_core(mine[2, 0]), swap_core(mine[2, 1])
    arrived_b = ring_y(add(rest[1], arrived_b).astype(BF))
    far_a = [("x", 2, dy) for dy in range(2)]
    far_b = [("z", (0, 2), dy, p) for dy in range(2) for p in range(2)]
    keys = [0, (2, 0), (2, 1)]
    carry = fold_of(list(zip(far_a, far_b[:2])), keys, [], carry, False)
    grad_tokens, shard_weights, keys_out = fold_of(
        list(zip(far_b, far_b[2:] + far_a)), keys, keys, carry, True
    )
    arrived_b, *crossed, keys_out = lax.optimization_barrier(
        (arrived_b, *crossed, keys_out)
    )
    grad_shard = add(rest[2], arrived_b, jnp.concatenate(crossed))
    shard_weights = shard_weights.reshape(512, COLS)

    return (
        outer_next[None, None],
        moment_next[None, None],
        shard_weights,
        keys_out,
        grad_tokens,
        grad_shard[None],
    )


def solution(mesh):
    fine = Mesh(mesh.devices.reshape(SIZES), AXES)
    rep, fsdp = ("x", "zh"), ("zl", "y", "c")
    return jax.shard_map(
        per_device,
        mesh=fine,
        in_specs=(
            P(rep, fsdp, None),
            P(fsdp, rep, None, None),
            P(fsdp, rep, None, None),
            P(AXES, None),
            P(AXES, None),
        ),
        out_specs=(
            P(fsdp, rep, None, None),
            P(fsdp, rep, None, None),
            P(fsdp, None),
            P(AXES, None),
            P(AXES, None),
            P(rep, fsdp, None),
        ),
        check_vma=False,
    )
```

```python
import functools
import itertools

import jax
import jax.numpy as jnp
import numpy as np
from jax import lax
from jax.experimental import pallas as pl
from jax.experimental.pallas import tpu as pltpu
from jax.sharding import Mesh, PartitionSpec as P

MOMENTUM_RATE = 0.9
OUTER_RATE = 0.7
AXES = ("x", "zh", "zl", "y", "c")
SIZES = (4, 2, 2, 4, 2)
TOK = 512
D = 8192
COLS = 1024
SCALE = D ** (-0.5)
VMEM = 24 * 1024 * 1024
ANY = pl.BlockSpec(memory_space=pl.ANY)
BF = jnp.bfloat16
F32 = jnp.float32


def permute(value, to):
    pairs = []
    for x, zh, zl, y, c in itertools.product(*[range(n) for n in SIZES]):
        tx, tz, ty, tc = to(x, zh * 2 + zl, y, c)
        tz = tz % 4
        target = (tx % 4, tz // 2, tz % 2, ty % 4, tc % 2)
        pairs.append(
            (
                int(np.ravel_multi_index((x, zh, zl, y, c), SIZES)),
                int(np.ravel_multi_index(target, SIZES)),
            )
        )
    return lax.ppermute(value, AXES, pairs)


def swap_core(value):
    return permute(value, lambda x, z, y, c: (x, z, y, 1 - c))


def ring_y(value):
    return permute(value, lambda x, z, y, c: (x, z, y + 1 - 2 * c, c))


def params(**more):
    return pltpu.CompilerParams(vmem_limit_bytes=VMEM, **more)


def half_kernel(at, tokens, out, held, in_sem, out_sem):
    c = at[4]
    loads = [
        pltpu.make_async_copy(
            tokens.at[:, pl.ds(pl.multiple_of((2 * g + 1 - c) * 512, 512), 512)],
            held.at[:, pl.ds(g * 512, 512)],
            in_sem.at[g],
        )
        for g in range(8)
    ]
    stores = [
        pltpu.make_async_copy(
            held.at[:, pl.ds(g * 512, 512)],
            out.at[:, pl.ds(g * 512, 512)],
            out_sem.at[g],
        )
        for g in range(8)
    ]
    for load in loads:
        load.start()
    for load, store in zip(loads, stores):
        load.wait()
        store.start()
    for store in stores:
        store.wait()


def other_half(at, tokens):
    return pl.pallas_call(
        half_kernel,
        out_shape=jax.ShapeDtypeStruct((TOK, D // 2), BF),
        in_specs=[pl.BlockSpec(memory_space=pltpu.SMEM), ANY],
        out_specs=ANY,
        scratch_shapes=[
            pltpu.VMEM((TOK, D // 2), BF),
            pltpu.SemaphoreType.DMA((8,)),
            pltpu.SemaphoreType.DMA((8,)),
        ],
        compiler_params=params(),
        cost_estimate=pl.CostEstimate(
            flops=0, bytes_accessed=2 * TOK * D, transcendentals=0
        ),
        name="half",
    )(at, tokens)


def grad_kernel(adds, blocks, mine, theirs, cot, cot_theirs, *refs):
    arrived, (out, *rest) = refs[:adds], refs[adds:]
    dims = (((0,), (0,)), ((), ()))
    total = lax.dot_general(mine[...], cot[...], dims, preferred_element_type=F32)
    total += lax.dot_general(
        theirs[...], cot_theirs[...], dims, preferred_element_type=F32
    )
    total = total * SCALE

    @pl.when(pl.program_id(0) == 0)
    def _():
        first = total
        for part in arrived:
            first = first + part[...].astype(F32)
        out[...] = first.astype(BF)

    for more in rest:

        @pl.when(pl.program_id(0) > 0)
        def _(more=more):
            more[0] = total.astype(BF)


def grad_blocks(blocks, core, tokens, tokens_theirs, cot, cot_theirs, arrived):
    count = len(blocks)
    table = jnp.stack([2 * g + core for g in blocks] + blocks).astype(jnp.int32)
    whole = pl.BlockSpec((TOK, COLS), lambda m, b: (0, 0))
    return pl.pallas_call(
        functools.partial(grad_kernel, len(arrived)),
        out_shape=[
            jax.ShapeDtypeStruct((512, COLS), BF),
            jax.ShapeDtypeStruct((count - 1, 512, COLS), BF),
        ][: min(count, 2)],
        grid_spec=pltpu.PrefetchScalarGridSpec(
            num_scalar_prefetch=1,
            grid=(count,),
            in_specs=[
                pl.BlockSpec((TOK, 512), lambda m, b: (0, b[m])),
                pl.BlockSpec((TOK, 512), lambda m, b: (0, b[count + m])),
                whole,
                whole,
            ]
            + [whole] * len(arrived),
            out_specs=[
                whole,
                pl.BlockSpec((1, 512, COLS), lambda m, b: (jnp.maximum(m - 1, 0), 0, 0)),
            ][: min(count, 2)],
        ),
        compiler_params=params(),
        cost_estimate=pl.CostEstimate(
            flops=count * 4 * TOK * 512 * COLS,
            bytes_accessed=(count * 2 + 2) << 20,
            transcendentals=0,
        ),
        name="grad",
    )(table, tokens, tokens_theirs, cot, cot_theirs, *arrived)


OFFSETS = (0, -1, 2, 1)


def fold_kernel(groups, mine, theirs, first, last, *refs):
    refs = list(refs)
    at, tokens, cot = refs[:3]
    refs = refs[3:]
    mine = {key: refs.pop(0) for key in mine}
    theirs = {key: refs.pop(0) for key in theirs}
    if not first:
        acc_in, _, _ = refs.pop(0), refs.pop(0), refs.pop(0)
    grad_out, weights_out, key_out = refs.pop(0), refs.pop(0), refs.pop(0)
    w, tok, grad, cot_v, w_sem, tok_sem, out_sem, own_sem, cot_sem = refs[:9]
    acc = refs[9] if last else key_out
    x, z, y, c = at[0], at[1], at[2], at[4]

    def part(held, s, dy):
        return held[s, dy] if (s, dy) in held else held[s].at[dy]

    def x_of(s):
        return (x + OFFSETS[s] + 4) & 3

    def z_of(s):
        return (z + OFFSETS[s] + 4) & 3

    def columns_of(group):
        if group[0] == "x":
            _, s, dy = group
            return [
                (
                    (zl * 8 + ((y + dy) & 3) * 2 + p) * 512 + x_of(s) * 128,
                    (zl * 2 + p) * 128,
                    128,
                )
                for zl in range(2)
                for p in range(2)
            ]
        _, (s, t), dy, p = group
        return [(((z_of(s) & 1) * 8 + ((y + 2 + dy) & 3) * 2 + p) * 512, 0, 512)]

    def load_weights(group, slot):
        def start(held):
            if group[0] == "x":
                _, s, dy = group
                for zl, zh in itertools.product(range(2), range(2)):
                    pltpu.make_async_copy(
                        part(held, s, dy).at[zh * 2 + zl],
                        w.at[slot, pl.ds(zl * 2, 2), zh],
                        w_sem.at[slot],
                    ).start()
            else:
                _, pair, dy, p = group
                for s in pair:
                    pltpu.make_async_copy(
                        part(held, s, dy).at[:, p],
                        w.at[slot, :, z_of(s) >> 1],
                        w_sem.at[slot],
                    ).start()

        here = 0 if group[0] == "x" else 1
        @pl.when(c == here)
        def _():
            start(mine)

        @pl.when(c != here)
        def _():
            start(theirs)

    count = len(groups)

    def loads(i):
        slot = i % 3
        load_weights(groups[i], slot)
        for a, b, n in columns_of(groups[i]):
            pltpu.make_async_copy(
                tokens.at[:, pl.ds(pl.multiple_of(a, 128), n)],
                tok.at[slot, :, pl.ds(b, n)],
                tok_sem.at[slot],
            ).start()

    def holds_own(group):
        return group[0] == "x" and group[2] == 0

    def weights_store(i):
        slot = i % 3
        return pltpu.make_async_copy(
            w.at[slot, (z & 1) * 2 + c],
            weights_out.at[x_of(groups[i][1])],
            own_sem.at[slot],
        )

    def stores(i):
        slot = i % 3
        for a, b, n in columns_of(groups[i]):
            pltpu.make_async_copy(
                grad.at[slot, :, pl.ds(b, n)],
                grad_out.at[:, pl.ds(pl.multiple_of(a, 128), n)],
                out_sem.at[slot],
            ).start()

    def whole(buffer, sem, slot):
        return pltpu.make_async_copy(buffer.at[slot], buffer.at[slot], sem.at[slot])

    cot_copy = pltpu.make_async_copy(cot, cot_v, cot_sem)
    cot_copy.start()
    loads(0)
    loads(1)
    if first:
        acc[...] = jnp.zeros_like(acc)
    else:
        acc[...] = acc_in[...]
    cot_copy.wait()

    @pl.loop(0, count)
    def _(i):
        slot = lax.rem(i, 3)
        for k in range(2, count):

            @pl.when(i + 2 == k)
            def _(k=k):
                loads(k)

        whole(w, w_sem, slot).wait()
        for k in range(count):
            if holds_own(groups[k]):

                @pl.when(i == k)
                def _(k=k):
                    weights_store(k).start()

        @pl.when(i >= 3)
        def _():
            whole(grad, out_sem, slot).wait()

        rows = w[slot].reshape(512, COLS)
        out = lax.dot_general(
            cot_v[...], rows, (((1,), (1,)), ((), ())), preferred_element_type=F32
        )
        grad[slot] = (out * SCALE).astype(BF)
        for k in range(count):

            @pl.when(i == k)
            def _(k=k):
                stores(k)

        whole(tok, tok_sem, slot).wait()
        acc[...] += jnp.dot(tok[slot], rows, preferred_element_type=F32)
        for k in range(count):
            if holds_own(groups[k]):

                @pl.when(i == k)
                def _(k=k):
                    weights_store(k).wait()

    if last:
        key_out[...] = (acc[...] * SCALE).astype(BF)
    for i in range(max(count - 3, 0), count):
        whole(grad, out_sem, i % 3).wait()


def fold(at, tokens, cot, groups, mine, theirs, carry, last):
    first = carry is None
    operands = [at, tokens, cot, *mine.values(), *theirs.values()]
    aliases = {}
    if not first:
        operands += [carry[2]]
        aliases = {len(operands): 0, len(operands) + 1: 1}
        operands += carry[:2]
    shapes = [
        jax.ShapeDtypeStruct((TOK, D), BF),
        jax.ShapeDtypeStruct((4, 2, 64, COLS), BF),
        jax.ShapeDtypeStruct((TOK, COLS), BF if last else F32),
    ]
    dma = pltpu.SemaphoreType.DMA
    scratch = [
        pltpu.VMEM((3, 4, 2, 64, COLS), BF),
        pltpu.VMEM((3, TOK, 512), BF),
        pltpu.VMEM((3, TOK, 512), BF),
        pltpu.VMEM((TOK, COLS), BF),
        dma((3,)),
        dma((3,)),
        dma((3,)),
        dma((3,)),
        dma(()),
    ]
    if last:
        scratch += [pltpu.VMEM((TOK, COLS), F32)]
    in_vmem = pl.BlockSpec(memory_space=pltpu.VMEM)
    in_specs = [pl.BlockSpec(memory_space=pltpu.SMEM)] + [ANY] * (len(operands) - 1)
    if not first:
        in_specs[-3] = in_vmem
    def kernel(*refs):
        fold_kernel(groups, list(mine), list(theirs), first, last, *refs)

    return pl.pallas_call(
        kernel,
        out_shape=shapes,
        in_specs=in_specs,
        out_specs=[ANY, ANY, in_vmem],
        scratch_shapes=scratch,
        input_output_aliases=aliases,
        compiler_params=params(),
        cost_estimate=pl.CostEstimate(
            flops=0, bytes_accessed=1 << 20,
            transcendentals=0,
        ),
        name="fold",
    )(*operands)


def per_device(deltas, outer_weights, momentum, tokens, key_cot):
    x, zh, zl, y, c = [lax.axis_index(a) for a in AXES]
    z = zh * 2 + zl
    way = 1 - 2 * c
    at = jnp.stack([x, z, y, zl, c]).astype(jnp.int32)
    blocks = deltas[0]

    tokens_theirs = swap_core(other_half(at, tokens))
    cot_theirs = swap_core(key_cot)

    def grads(which, tokens_theirs, *arrived):
        blocks = [
            (zl if half else 1 - zl) * 4 + ((y - way * (s + 1) + 8) & 3)
            for half, s in which
        ]
        return grad_blocks(
            blocks, c, tokens, tokens_theirs, key_cot, cot_theirs, arrived
        )

    def add(*parts):
        total = parts[0].astype(F32)
        for part in parts[1:]:
            total = total + part.astype(F32)
        return total

    by_x = blocks.reshape(4, 2, 64, COLS)
    got = []
    for d in (2, 1, 3):
        piece = lax.dynamic_index_in_dim(by_x, (x + d) & 3, 0, False)
        got.append(permute(piece, lambda px, pz, py, pc: (px + d, pz, py, pc)))
    first, first_b = grads([(0, 0), (1, 0)], tokens_theirs)
    *got, first, first_b = lax.optimization_barrier((*got, first, first_b[0]))
    arrived = ring_y(first)
    part = add(lax.dynamic_index_in_dim(by_x, x, 0, False), *got)
    crossing = lax.dynamic_index_in_dim(part, 1 - zh, 0, False).astype(BF)
    crossing = permute(crossing, lambda px, pz, py, pc: (px, pz + 2, py, pc))
    summed = add(lax.dynamic_index_in_dim(part, zh, 0, False), crossing)
    mean_delta = summed / 8
    moment_next = MOMENTUM_RATE * momentum[0, 0] + mean_delta
    outer_next = outer_weights[0, 0] - OUTER_RATE * (
        mean_delta + MOMENTUM_RATE * moment_next
    )
    owned = outer_next.astype(BF)

    def short_way(value, d):
        return permute(
            value,
            lambda px, pz, py, pc: (px - d * pc, pz - d * (1 - pc), py, pc),
        )

    def long_way(value, d):
        return permute(
            value,
            lambda px, pz, py, pc: (px + d * (1 - pc), pz + d * pc, py, pc),
        )

    def in_order(parts, here):
        whole = jnp.zeros((2, 4, 2, 64, COLS), BF)
        for d, part in enumerate(parts):
            whole = lax.dynamic_update_slice_in_dim(
                whole, part[:, None], (here + d) & 3, 1
            )
        return whole

    other, arrived = lax.optimization_barrier((swap_core(owned), arrived))
    both = jnp.where(c == 0, jnp.stack([owned, other]), jnp.stack([other, owned]))
    near = permute(both, lambda px, pz, py, pc: (px, pz, py - 1 + 2 * pc, pc))
    far = permute(both, lambda px, pz, py, pc: (px, pz, py + 2 * pc, pc))
    c0 = jnp.stack([far, near])
    c0, first_b, late = lax.optimization_barrier((c0, first_b, tokens_theirs))
    arrived_b = ring_y(first_b)
    second, second_b = grads([(0, 1), (1, 1)], late, arrived)
    parts = [short_way(c0, d) for d in (1, 2, 3)]
    arrived = ring_y(second)
    second_b = second_b[0]
    c1 = in_order([c0] + parts, jnp.where(c == 0, z, x))
    c1, late = lax.optimization_barrier((c1, late))
    third, rest = grads([(0, 2), (0, 3), (1, 2), (1, 3)], late, arrived)

    mine, theirs = {0: c1}, {0: swap_core(c1)}
    mine[1], mine[3] = long_way(c1, 1), long_way(c1, -1)

    def fold_of(groups, keys, carry, last):
        return fold(
            at, tokens, key_cot, groups,
            {k: mine[k] for k in keys}, {k: theirs[k] for k in keys}, carry, last,
        )

    carry = fold_of([("x", 0, 0), ("x", 0, 1)], [0], None, False)
    arrived = ring_y(third)
    mine[1], mine[3], arrived, arrived_b, *carry = lax.optimization_barrier(
        (mine[1], mine[3], arrived, arrived_b, *carry)
    )
    mine[2, 0] = long_way(mine[1][0], 1)
    mine[2, 1] = long_way(mine[3][1], -1)
    theirs[1], theirs[3] = swap_core(mine[1]), swap_core(mine[3])
    crossed = add(rest[0], arrived).astype(BF)
    crossed = [
        permute(half, lambda px, pz, py, pc: (px, pz ^ 1, py, pc))
        for half in (crossed[:192], crossed[192:])
    ]
    arrived_b = ring_y(add(second_b, arrived_b).astype(BF))
    groups = [("x", s, dy) for s in (1, 3) for dy in range(2)]
    groups += [("z", (1, 3), dy, p) for dy in range(2) for p in range(2)]
    carry = fold_of(groups, [1, 3], carry, False)
    mine[2, 0], mine[2, 1], arrived_b, crossed[0], *carry = lax.optimization_barrier(
        (mine[2, 0], mine[2, 1], arrived_b, crossed[0], *carry)
    )
    theirs[2, 0], theirs[2, 1] = swap_core(mine[2, 0]), swap_core(mine[2, 1])
    arrived_b = ring_y(add(rest[1], arrived_b).astype(BF))
    groups = [("x", 2, dy) for dy in range(2)]
    groups += [("z", (0, 2), dy, p) for dy in range(2) for p in range(2)]
    grad_tokens, shard_weights, keys_out = fold_of(
        groups, [0, (2, 0), (2, 1)], carry, True
    )
    arrived_b, *crossed, keys_out = lax.optimization_barrier(
        (arrived_b, *crossed, keys_out)
    )
    grad_shard = add(rest[2], arrived_b, jnp.concatenate(crossed))
    shard_weights = shard_weights.reshape(512, COLS)

    return (
        outer_next[None, None],
        moment_next[None, None],
        shard_weights,
        keys_out,
        grad_tokens,
        grad_shard[None],
    )


def solution(mesh):
    fine = Mesh(mesh.devices.reshape(SIZES), AXES)
    rep, fsdp = ("x", "zh"), ("zl", "y", "c")
    return jax.shard_map(
        per_device,
        mesh=fine,
        in_specs=(
            P(rep, fsdp, None),
            P(fsdp, rep, None, None),
            P(fsdp, rep, None, None),
            P(AXES, None),
            P(AXES, None),
        ),
        out_specs=(
            P(fsdp, rep, None, None),
            P(fsdp, rep, None, None),
            P(fsdp, None),
            P(AXES, None),
            P(AXES, None),
            P(rep, fsdp, None),
        ),
        check_vma=False,
    )
```

```python
import functools
import itertools

import jax
import jax.numpy as jnp
import numpy as np
from jax import lax
from jax.experimental import pallas as pl
from jax.experimental.pallas import tpu as pltpu
from jax.sharding import Mesh, PartitionSpec as P

MOMENTUM_RATE = 0.9
OUTER_RATE = 0.7
AXES = ("x", "zh", "zl", "y", "c")
SIZES = (4, 2, 2, 4, 2)
TOK = 512
D = 8192
COLS = 1024
SCALE = D ** (-0.5)
VMEM = 48 * 1024 * 1024
FOLD_VMEM = 40 * 1024 * 1024
ANY = pl.BlockSpec(memory_space=pl.ANY)
BF = jnp.bfloat16
F32 = jnp.float32


def permute(value, to):
    pairs = []
    for x, zh, zl, y, c in itertools.product(*[range(n) for n in SIZES]):
        tx, tz, ty, tc = to(x, zh * 2 + zl, y, c)
        tz = tz % 4
        target = (tx % 4, tz // 2, tz % 2, ty % 4, tc % 2)
        pairs.append(
            (
                int(np.ravel_multi_index((x, zh, zl, y, c), SIZES)),
                int(np.ravel_multi_index(target, SIZES)),
            )
        )
    return lax.ppermute(value, AXES, pairs)


def swap_core(value):
    return permute(value, lambda x, z, y, c: (x, z, y, 1 - c))


def ring_y(value):
    return permute(value, lambda x, z, y, c: (x, z, y + 1 - 2 * c, c))


def params(limit=VMEM):
    return pltpu.CompilerParams(vmem_limit_bytes=limit)


def half_kernel(at, tokens, out, held, in_sem, out_sem):
    c = at[4]
    loads = [
        pltpu.make_async_copy(
            tokens.at[:, pl.ds(pl.multiple_of((2 * g + 1 - c) * 512, 512), 512)],
            held.at[:, pl.ds(g * 512, 512)],
            in_sem.at[g],
        )
        for g in range(8)
    ]
    stores = [
        pltpu.make_async_copy(
            held.at[:, pl.ds(g * 512, 512)],
            out.at[:, pl.ds(g * 512, 512)],
            out_sem.at[g],
        )
        for g in range(8)
    ]
    for load in loads:
        load.start()
    for load, store in zip(loads, stores):
        load.wait()
        store.start()
    for store in stores:
        store.wait()


def other_half(at, tokens):
    return pl.pallas_call(
        half_kernel,
        out_shape=jax.ShapeDtypeStruct((TOK, D // 2), BF),
        in_specs=[pl.BlockSpec(memory_space=pltpu.SMEM), ANY],
        out_specs=ANY,
        scratch_shapes=[
            pltpu.VMEM((TOK, D // 2), BF),
            pltpu.SemaphoreType.DMA((8,)),
            pltpu.SemaphoreType.DMA((8,)),
        ],
        compiler_params=params(),
        cost_estimate=pl.CostEstimate(
            flops=0, bytes_accessed=2 * TOK * D, transcendentals=0
        ),
        name="half",
    )(at, tokens)


def grad_kernel(adds, blocks, mine, theirs, cot, cot_theirs, *refs):
    arrived, (out, *rest) = refs[:adds], refs[adds:]
    dims = (((0,), (0,)), ((), ()))
    total = lax.dot_general(mine[...], cot[...], dims, preferred_element_type=F32)
    total += lax.dot_general(
        theirs[...], cot_theirs[...], dims, preferred_element_type=F32
    )
    total = total * SCALE

    @pl.when(pl.program_id(0) == 0)
    def _():
        first = total
        for part in arrived:
            first = first + part[...].astype(F32)
        out[...] = first.astype(BF)

    for more in rest:

        @pl.when(pl.program_id(0) > 0)
        def _(more=more):
            more[0] = total.astype(BF)


def grad_blocks(blocks, core, tokens, tokens_theirs, cot, cot_theirs, arrived):
    count = len(blocks)
    table = jnp.stack([2 * g + core for g in blocks] + blocks).astype(jnp.int32)
    whole = pl.BlockSpec((TOK, COLS), lambda m, b: (0, 0))
    return pl.pallas_call(
        functools.partial(grad_kernel, len(arrived)),
        out_shape=[
            jax.ShapeDtypeStruct((512, COLS), BF),
            jax.ShapeDtypeStruct((count - 1, 512, COLS), BF),
        ][: min(count, 2)],
        grid_spec=pltpu.PrefetchScalarGridSpec(
            num_scalar_prefetch=1,
            grid=(count,),
            in_specs=[
                pl.BlockSpec((TOK, 512), lambda m, b: (0, b[m])),
                pl.BlockSpec((TOK, 512), lambda m, b: (0, b[count + m])),
                whole,
                whole,
            ]
            + [whole] * len(arrived),
            out_specs=[
                whole,
                pl.BlockSpec((1, 512, COLS), lambda m, b: (jnp.maximum(m - 1, 0), 0, 0)),
            ][: min(count, 2)],
        ),
        compiler_params=params(),
        cost_estimate=pl.CostEstimate(
            flops=count * 4 * TOK * 512 * COLS,
            bytes_accessed=(count * 2 + 2) << 20,
            transcendentals=0,
        ),
        name="grad",
    )(table, tokens, tokens_theirs, cot, cot_theirs, *arrived)


OFFSETS = (0, -1, 2, 1)


def fold_kernel(groups, mine, theirs, first, last, *refs):
    refs = list(refs)
    at, tokens, cot = refs[:3]
    refs = refs[3:]
    mine = {key: refs.pop(0) for key in mine}
    theirs = {key: refs.pop(0) for key in theirs}
    if not first:
        acc_in, _, _ = refs.pop(0), refs.pop(0), refs.pop(0)
    grad_out, weights_out, key_out = refs.pop(0), refs.pop(0), refs.pop(0)
    w, tok, grad, cot_v, w_sem, tok_sem, out_sem, own_sem, cot_sem = refs[:9]
    acc = refs[9] if last else key_out
    x, z, y, c = at[0], at[1], at[2], at[4]

    def part(held, s, dy):
        return held[s, dy] if (s, dy) in held else held[s].at[dy]

    def x_of(s):
        return (x + OFFSETS[s] + 4) & 3

    def z_of(s):
        return (z + OFFSETS[s] + 4) & 3

    def columns_of(group):
        if group[0] == "x":
            _, s, dy = group
            return [
                (
                    (zl * 8 + ((y + dy) & 3) * 2 + p) * 512 + x_of(s) * 128,
                    (zl * 2 + p) * 128,
                    128,
                )
                for zl in range(2)
                for p in range(2)
            ]
        _, (s, t), dy, p = group
        return [(((z_of(s) & 1) * 8 + ((y + 2 + dy) & 3) * 2 + p) * 512, 0, 512)]

    def load_weights(group, slot):
        def start(held):
            if group[0] == "x":
                _, s, dy = group
                for zl, zh in itertools.product(range(2), range(2)):
                    pltpu.make_async_copy(
                        part(held, s, dy).at[zh * 2 + zl],
                        w.at[slot, pl.ds(zl * 2, 2), zh],
                        w_sem.at[slot],
                    ).start()
            else:
                _, pair, dy, p = group
                for s in pair:
                    pltpu.make_async_copy(
                        part(held, s, dy).at[:, p],
                        w.at[slot, :, z_of(s) >> 1],
                        w_sem.at[slot],
                    ).start()

        here = 0 if group[0] == "x" else 1
        @pl.when(c == here)
        def _():
            start(mine)

        @pl.when(c != here)
        def _():
            start(theirs)

    count = len(groups)

    def loads(i):
        slot = i % 3
        load_weights(groups[i], slot)
        for a, b, n in columns_of(groups[i]):
            pltpu.make_async_copy(
                tokens.at[:, pl.ds(pl.multiple_of(a, 128), n)],
                tok.at[slot, :, pl.ds(b, n)],
                tok_sem.at[slot],
            ).start()

    def holds_own(group):
        return group[0] == "x" and group[2] == 0

    def weights_store(i):
        slot = i % 3
        return pltpu.make_async_copy(
            w.at[slot, (z & 1) * 2 + c],
            weights_out.at[x_of(groups[i][1])],
            own_sem.at[slot],
        )

    def stores(i):
        slot = i % 3
        for a, b, n in columns_of(groups[i]):
            pltpu.make_async_copy(
                grad.at[slot, :, pl.ds(b, n)],
                grad_out.at[:, pl.ds(pl.multiple_of(a, 128), n)],
                out_sem.at[slot],
            ).start()

    def whole(buffer, sem, slot):
        return pltpu.make_async_copy(buffer.at[slot], buffer.at[slot], sem.at[slot])

    cot_copy = pltpu.make_async_copy(cot, cot_v, cot_sem)
    cot_copy.start()
    loads(0)
    loads(1)
    if first:
        acc[...] = jnp.zeros_like(acc)
    else:
        acc[...] = acc_in[...]
    cot_copy.wait()

    @pl.loop(0, count)
    def _(i):
        slot = lax.rem(i, 3)
        for k in range(2, count):

            @pl.when(i + 2 == k)
            def _(k=k):
                loads(k)

        whole(w, w_sem, slot).wait()
        for k in range(count):
            if holds_own(groups[k]):

                @pl.when(i == k)
                def _(k=k):
                    weights_store(k).start()

        @pl.when(i >= 3)
        def _():
            whole(grad, out_sem, slot).wait()

        rows = w[slot].reshape(512, COLS)
        out = lax.dot_general(
            cot_v[...], rows, (((1,), (1,)), ((), ())), preferred_element_type=F32
        )
        grad[slot] = (out * SCALE).astype(BF)
        for k in range(count):

            @pl.when(i == k)
            def _(k=k):
                stores(k)

        whole(tok, tok_sem, slot).wait()
        acc[...] += jnp.dot(tok[slot], rows, preferred_element_type=F32)
        for k in range(count):
            if holds_own(groups[k]):

                @pl.when(i == k)
                def _(k=k):
                    weights_store(k).wait()

    if last:
        key_out[...] = (acc[...] * SCALE).astype(BF)
    for i in range(max(count - 3, 0), count):
        whole(grad, out_sem, i % 3).wait()


def fold(at, tokens, cot, groups, mine, theirs, carry, last):
    first = carry is None
    operands = [at, tokens, cot, *mine.values(), *theirs.values()]
    aliases = {}
    if not first:
        operands += [carry[2]]
        aliases = {len(operands): 0, len(operands) + 1: 1}
        operands += carry[:2]
    shapes = [
        jax.ShapeDtypeStruct((TOK, D), BF),
        jax.ShapeDtypeStruct((4, 2, 64, COLS), BF),
        jax.ShapeDtypeStruct((TOK, COLS), BF if last else F32),
    ]
    dma = pltpu.SemaphoreType.DMA
    scratch = [
        pltpu.VMEM((3, 4, 2, 64, COLS), BF),
        pltpu.VMEM((3, TOK, 512), BF),
        pltpu.VMEM((3, TOK, 512), BF),
        pltpu.VMEM((TOK, COLS), BF),
        dma((3,)),
        dma((3,)),
        dma((3,)),
        dma((3,)),
        dma(()),
    ]
    if last:
        scratch += [pltpu.VMEM((TOK, COLS), F32)]
    in_vmem = pl.BlockSpec(memory_space=pltpu.VMEM)
    in_specs = [pl.BlockSpec(memory_space=pltpu.SMEM)] + [ANY] * (len(operands) - 1)
    if not first:
        in_specs[-3] = in_vmem
    def kernel(*refs):
        fold_kernel(groups, list(mine), list(theirs), first, last, *refs)

    return pl.pallas_call(
        kernel,
        out_shape=shapes,
        in_specs=in_specs,
        out_specs=[ANY, ANY, in_vmem],
        scratch_shapes=scratch,
        input_output_aliases=aliases,
        compiler_params=params(FOLD_VMEM),
        cost_estimate=pl.CostEstimate(
            flops=0, bytes_accessed=1 << 20,
            transcendentals=0,
        ),
        name="fold",
    )(*operands)


def per_device(deltas, outer_weights, momentum, tokens, key_cot):
    x, zh, zl, y, c = [lax.axis_index(a) for a in AXES]
    z = zh * 2 + zl
    way = 1 - 2 * c
    at = jnp.stack([x, z, y, zl, c]).astype(jnp.int32)
    blocks = deltas[0]

    tokens_theirs = swap_core(other_half(at, tokens))
    cot_theirs = swap_core(key_cot)

    def grads(which, tokens_theirs, *arrived):
        blocks = [
            (zl if half else 1 - zl) * 4 + ((y - way * (s + 1) + 8) & 3)
            for half, s in which
        ]
        return grad_blocks(
            blocks, c, tokens, tokens_theirs, key_cot, cot_theirs, arrived
        )

    def add(*parts):
        total = parts[0].astype(F32)
        for part in parts[1:]:
            total = total + part.astype(F32)
        return total

    by_x = blocks.reshape(4, 2, 64, COLS)
    got = []
    for d in (2, 1, 3):
        piece = lax.dynamic_index_in_dim(by_x, (x + d) & 3, 0, False)
        got.append(permute(piece, lambda px, pz, py, pc: (px + d, pz, py, pc)))
    first, first_b = grads([(0, 0), (1, 0)], tokens_theirs)
    *got, first, first_b = lax.optimization_barrier((*got, first, first_b[0]))
    arrived = ring_y(first)
    part = add(lax.dynamic_index_in_dim(by_x, x, 0, False), *got)
    crossing = lax.dynamic_index_in_dim(part, 1 - zh, 0, False).astype(BF)
    crossing = permute(crossing, lambda px, pz, py, pc: (px, pz + 2, py, pc))
    summed = add(lax.dynamic_index_in_dim(part, zh, 0, False), crossing)
    mean_delta = summed / 8
    moment_next = MOMENTUM_RATE * momentum[0, 0] + mean_delta
    outer_next = outer_weights[0, 0] - OUTER_RATE * (
        mean_delta + MOMENTUM_RATE * moment_next
    )
    owned = outer_next.astype(BF)

    def short_way(value, d):
        return permute(
            value,
            lambda px, pz, py, pc: (px - d * pc, pz - d * (1 - pc), py, pc),
        )

    def long_way(value, d):
        return permute(
            value,
            lambda px, pz, py, pc: (px + d * (1 - pc), pz + d * pc, py, pc),
        )

    def in_order(parts, here):
        whole = jnp.zeros((2, 4, 2, 64, COLS), BF)
        for d, part in enumerate(parts):
            whole = lax.dynamic_update_slice_in_dim(
                whole, part[:, None], (here + d) & 3, 1
            )
        return whole

    other, arrived = lax.optimization_barrier((swap_core(owned), arrived))
    both = jnp.where(c == 0, jnp.stack([owned, other]), jnp.stack([other, owned]))
    near = permute(both, lambda px, pz, py, pc: (px, pz, py - 1 + 2 * pc, pc))
    far = permute(both, lambda px, pz, py, pc: (px, pz, py + 2 * pc, pc))
    c0 = jnp.stack([far, near])
    c0, first_b, late = lax.optimization_barrier((c0, first_b, tokens_theirs))
    arrived_b = ring_y(first_b)
    second, second_b = grads([(0, 1), (1, 1)], late, arrived)
    parts = [short_way(c0, d) for d in (1, 2, 3)]
    arrived = ring_y(second)
    second_b = second_b[0]
    c1 = in_order([c0] + parts, jnp.where(c == 0, z, x))
    c1, late = lax.optimization_barrier((c1, late))
    third, rest = grads([(0, 2), (0, 3), (1, 2), (1, 3)], late, arrived)

    mine, theirs = {0: c1}, {0: swap_core(c1)}
    mine[1], mine[3] = long_way(c1, 1), long_way(c1, -1)

    def fold_of(groups, keys, carry, last):
        return fold(
            at, tokens, key_cot, groups,
            {k: mine[k] for k in keys}, {k: theirs[k] for k in keys}, carry, last,
        )

    carry = fold_of([("x", 0, 0), ("x", 0, 1)], [0], None, False)
    arrived = ring_y(third)
    mine[1], mine[3], arrived, arrived_b, *carry = lax.optimization_barrier(
        (mine[1], mine[3], arrived, arrived_b, *carry)
    )
    mine[2, 0] = long_way(mine[1][0], 1)
    mine[2, 1] = long_way(mine[3][1], -1)
    theirs[1], theirs[3] = swap_core(mine[1]), swap_core(mine[3])
    crossed = add(rest[0], arrived).astype(BF)
    crossed = [
        permute(half, lambda px, pz, py, pc: (px, pz ^ 1, py, pc))
        for half in (crossed[:192], crossed[192:])
    ]
    arrived_b = ring_y(add(second_b, arrived_b).astype(BF))
    groups = [("x", s, dy) for s in (1, 3) for dy in range(2)]
    groups += [("z", (1, 3), dy, p) for dy in range(2) for p in range(2)]
    carry = fold_of(groups, [1, 3], carry, False)
    mine[2, 0], mine[2, 1], arrived_b, crossed[0], *carry = lax.optimization_barrier(
        (mine[2, 0], mine[2, 1], arrived_b, crossed[0], *carry)
    )
    theirs[2, 0], theirs[2, 1] = swap_core(mine[2, 0]), swap_core(mine[2, 1])
    arrived_b = ring_y(add(rest[1], arrived_b).astype(BF))
    groups = [("x", 2, dy) for dy in range(2)]
    groups += [("z", (0, 2), dy, p) for dy in range(2) for p in range(2)]
    grad_tokens, shard_weights, keys_out = fold_of(
        groups, [0, (2, 0), (2, 1)], carry, True
    )
    arrived_b, *crossed, keys_out = lax.optimization_barrier(
        (arrived_b, *crossed, keys_out)
    )
    grad_shard = add(rest[2], arrived_b, jnp.concatenate(crossed))
    shard_weights = shard_weights.reshape(512, COLS)

    return (
        outer_next[None, None],
        moment_next[None, None],
        shard_weights,
        keys_out,
        grad_tokens,
        grad_shard[None],
    )


def solution(mesh):
    fine = Mesh(mesh.devices.reshape(SIZES), AXES)
    rep, fsdp = ("x", "zh"), ("zl", "y", "c")
    return jax.shard_map(
        per_device,
        mesh=fine,
        in_specs=(
            P(rep, fsdp, None),
            P(fsdp, rep, None, None),
            P(fsdp, rep, None, None),
            P(AXES, None),
            P(AXES, None),
        ),
        out_specs=(
            P(fsdp, rep, None, None),
            P(fsdp, rep, None, None),
            P(fsdp, None),
            P(AXES, None),
            P(AXES, None),
            P(rep, fsdp, None),
        ),
        check_vma=False,
    )
```

```python
import functools
import itertools

import jax
import jax.numpy as jnp
import numpy as np
from jax import lax
from jax.experimental import pallas as pl
from jax.experimental.pallas import tpu as pltpu
from jax.sharding import Mesh, PartitionSpec as P

MOMENTUM_RATE = 0.9
OUTER_RATE = 0.7
AXES = ("x", "zh", "zl", "y", "c")
SIZES = (4, 2, 2, 4, 2)
TOK = 512
D = 8192
COLS = 1024
SCALE = D ** (-0.5)
VMEM = 48 * 1024 * 1024
FOLD_VMEM = 40 * 1024 * 1024
ANY = pl.BlockSpec(memory_space=pl.ANY)
BF = jnp.bfloat16
F32 = jnp.float32


def permute(value, to):
    pairs = []
    for x, zh, zl, y, c in itertools.product(*[range(n) for n in SIZES]):
        tx, tz, ty, tc = to(x, zh * 2 + zl, y, c)
        tz = tz % 4
        target = (tx % 4, tz // 2, tz % 2, ty % 4, tc % 2)
        pairs.append(
            (
                int(np.ravel_multi_index((x, zh, zl, y, c), SIZES)),
                int(np.ravel_multi_index(target, SIZES)),
            )
        )
    return lax.ppermute(value, AXES, pairs)


def swap_core(value):
    return permute(value, lambda x, z, y, c: (x, z, y, 1 - c))


def ring_y(value):
    return permute(value, lambda x, z, y, c: (x, z, y + 1 - 2 * c, c))


def params(limit=VMEM):
    return pltpu.CompilerParams(vmem_limit_bytes=limit)


def half_kernel(at, tokens, out, held, in_sem, out_sem):
    c = at[4]
    loads = [
        pltpu.make_async_copy(
            tokens.at[:, pl.ds(pl.multiple_of((2 * g + 1 - c) * 512, 512), 512)],
            held.at[:, pl.ds(g * 512, 512)],
            in_sem.at[g],
        )
        for g in range(8)
    ]
    stores = [
        pltpu.make_async_copy(
            held.at[:, pl.ds(g * 512, 512)],
            out.at[:, pl.ds(g * 512, 512)],
            out_sem.at[g],
        )
        for g in range(8)
    ]
    for load in loads:
        load.start()
    for load, store in zip(loads, stores):
        load.wait()
        store.start()
    for store in stores:
        store.wait()


def other_half(at, tokens):
    return pl.pallas_call(
        half_kernel,
        out_shape=jax.ShapeDtypeStruct((TOK, D // 2), BF),
        in_specs=[pl.BlockSpec(memory_space=pltpu.SMEM), ANY],
        out_specs=ANY,
        scratch_shapes=[
            pltpu.VMEM((TOK, D // 2), BF),
            pltpu.SemaphoreType.DMA((8,)),
            pltpu.SemaphoreType.DMA((8,)),
        ],
        compiler_params=params(),
        cost_estimate=pl.CostEstimate(
            flops=0, bytes_accessed=2 * TOK * D, transcendentals=0
        ),
        name="half",
    )(at, tokens)


def grad_kernel(adds, blocks, mine, theirs, cot, cot_theirs, *refs):
    arrived, (out, *rest) = refs[:adds], refs[adds:]
    dims = (((0,), (0,)), ((), ()))
    total = lax.dot_general(mine[...], cot[...], dims, preferred_element_type=F32)
    total += lax.dot_general(
        theirs[...], cot_theirs[...], dims, preferred_element_type=F32
    )
    total = total * SCALE

    @pl.when(pl.program_id(0) == 0)
    def _():
        first = total
        for part in arrived:
            first = first + part[...].astype(F32)
        out[...] = first.astype(BF)

    for more in rest:

        @pl.when(pl.program_id(0) > 0)
        def _(more=more):
            more[0] = total.astype(BF)


def grad_blocks(blocks, core, tokens, tokens_theirs, cot, cot_theirs, arrived):
    count = len(blocks)
    table = jnp.stack([2 * g + core for g in blocks] + blocks).astype(jnp.int32)
    whole = pl.BlockSpec((TOK, COLS), lambda m, b: (0, 0))
    return pl.pallas_call(
        functools.partial(grad_kernel, len(arrived)),
        out_shape=[
            jax.ShapeDtypeStruct((512, COLS), BF),
            jax.ShapeDtypeStruct((count - 1, 512, COLS), BF),
        ][: min(count, 2)],
        grid_spec=pltpu.PrefetchScalarGridSpec(
            num_scalar_prefetch=1,
            grid=(count,),
            in_specs=[
                pl.BlockSpec((TOK, 512), lambda m, b: (0, b[m])),
                pl.BlockSpec((TOK, 512), lambda m, b: (0, b[count + m])),
                whole,
                whole,
            ]
            + [whole] * len(arrived),
            out_specs=[
                whole,
                pl.BlockSpec((1, 512, COLS), lambda m, b: (jnp.maximum(m - 1, 0), 0, 0)),
            ][: min(count, 2)],
        ),
        compiler_params=params(),
        cost_estimate=pl.CostEstimate(
            flops=count * 4 * TOK * 512 * COLS,
            bytes_accessed=(count * 2 + 2) << 20,
            transcendentals=0,
        ),
        name="grad",
    )(table, tokens, tokens_theirs, cot, cot_theirs, *arrived)


OFFSETS = (0, -1, 2, 1)


def fold_kernel(groups, mine, theirs, first, last, *refs):
    refs = list(refs)
    at, tokens, cot = refs[:3]
    refs = refs[3:]
    mine = {key: refs.pop(0) for key in mine}
    theirs = {key: refs.pop(0) for key in theirs}
    if not first:
        acc_in, _, _ = refs.pop(0), refs.pop(0), refs.pop(0)
    grad_out, weights_out, key_out = refs.pop(0), refs.pop(0), refs.pop(0)
    w, tok, grad, cot_v, w_sem, tok_sem, out_sem, own_sem, cot_sem = refs[:9]
    acc = refs[9] if last else key_out
    x, z, y, c = at[0], at[1], at[2], at[4]

    def part(held, s, dy):
        return held[s, dy] if (s, dy) in held else held[s].at[dy]

    def x_of(s):
        return (x + OFFSETS[s] + 4) & 3

    def z_of(s):
        return (z + OFFSETS[s] + 4) & 3

    def columns_of(group):
        if group[0] == "x":
            _, s, dy = group
            return [
                (
                    (zl * 8 + ((y + dy) & 3) * 2 + p) * 512 + x_of(s) * 128,
                    (zl * 2 + p) * 128,
                    128,
                )
                for zl in range(2)
                for p in range(2)
            ]
        _, (s, t), dy, p = group
        return [(((z_of(s) & 1) * 8 + ((y + 2 + dy) & 3) * 2 + p) * 512, 0, 512)]

    def load_weights(group, slot):
        def start(held):
            if group[0] == "x":
                _, s, dy = group
                for zl, zh in itertools.product(range(2), range(2)):
                    pltpu.make_async_copy(
                        part(held, s, dy).at[zh * 2 + zl],
                        w.at[slot, pl.ds(zl * 2, 2), zh],
                        w_sem.at[slot],
                    ).start()
            else:
                _, pair, dy, p = group
                for s in pair:
                    pltpu.make_async_copy(
                        part(held, s, dy).at[:, p],
                        w.at[slot, :, z_of(s) >> 1],
                        w_sem.at[slot],
                    ).start()

        here = 0 if group[0] == "x" else 1
        @pl.when(c == here)
        def _():
            start(mine)

        @pl.when(c != here)
        def _():
            start(theirs)

    count = len(groups)

    def loads(i):
        slot = i % 3
        load_weights(groups[i], slot)
        for a, b, n in columns_of(groups[i]):
            pltpu.make_async_copy(
                tokens.at[:, pl.ds(pl.multiple_of(a, 128), n)],
                tok.at[slot, :, pl.ds(b, n)],
                tok_sem.at[slot],
            ).start()

    def holds_own(group):
        return group[0] == "x" and group[2] == 0

    def weights_store(i):
        slot = i % 3
        return pltpu.make_async_copy(
            w.at[slot, (z & 1) * 2 + c],
            weights_out.at[x_of(groups[i][1])],
            own_sem.at[slot],
        )

    def stores(i):
        slot = i % 3
        for a, b, n in columns_of(groups[i]):
            pltpu.make_async_copy(
                grad.at[slot, :, pl.ds(b, n)],
                grad_out.at[:, pl.ds(pl.multiple_of(a, 128), n)],
                out_sem.at[slot],
            ).start()

    def whole(buffer, sem, slot):
        return pltpu.make_async_copy(buffer.at[slot], buffer.at[slot], sem.at[slot])

    cot_copy = pltpu.make_async_copy(cot, cot_v, cot_sem)
    cot_copy.start()
    loads(0)
    loads(1)
    if first:
        acc[...] = jnp.zeros_like(acc)
    else:
        acc[...] = acc_in[...]
    cot_copy.wait()

    @pl.loop(0, count)
    def _(i):
        slot = lax.rem(i, 3)
        for k in range(2, count):

            @pl.when(i + 2 == k)
            def _(k=k):
                loads(k)

        whole(w, w_sem, slot).wait()
        for k in range(count):
            if holds_own(groups[k]):

                @pl.when(i == k)
                def _(k=k):
                    weights_store(k).start()

        @pl.when(i >= 3)
        def _():
            whole(grad, out_sem, slot).wait()

        rows = w[slot].reshape(512, COLS)
        out = lax.dot_general(
            cot_v[...], rows, (((1,), (1,)), ((), ())), preferred_element_type=F32
        )
        grad[slot] = (out * SCALE).astype(BF)
        for k in range(count):

            @pl.when(i == k)
            def _(k=k):
                stores(k)

        whole(tok, tok_sem, slot).wait()
        acc[...] += jnp.dot(tok[slot], rows, preferred_element_type=F32)
        for k in range(count):
            if holds_own(groups[k]):

                @pl.when(i == k)
                def _(k=k):
                    weights_store(k).wait()

    if last:
        key_out[...] = (acc[...] * SCALE).astype(BF)
    for i in range(max(count - 3, 0), count):
        whole(grad, out_sem, i % 3).wait()


def fold(at, tokens, cot, groups, mine, theirs, carry, last):
    first = carry is None
    operands = [at, tokens, cot, *mine.values(), *theirs.values()]
    aliases = {}
    if not first:
        operands += [carry[2]]
        aliases = {len(operands): 0, len(operands) + 1: 1}
        operands += carry[:2]
    shapes = [
        jax.ShapeDtypeStruct((TOK, D), BF),
        jax.ShapeDtypeStruct((4, 2, 64, COLS), BF),
        jax.ShapeDtypeStruct((TOK, COLS), BF if last else F32),
    ]
    dma = pltpu.SemaphoreType.DMA
    scratch = [
        pltpu.VMEM((3, 4, 2, 64, COLS), BF),
        pltpu.VMEM((3, TOK, 512), BF),
        pltpu.VMEM((3, TOK, 512), BF),
        pltpu.VMEM((TOK, COLS), BF),
        dma((3,)),
        dma((3,)),
        dma((3,)),
        dma((3,)),
        dma(()),
    ]
    if last:
        scratch += [pltpu.VMEM((TOK, COLS), F32)]
    in_vmem = pl.BlockSpec(memory_space=pltpu.VMEM)
    in_specs = [pl.BlockSpec(memory_space=pltpu.SMEM)] + [ANY] * (len(operands) - 1)
    if not first:
        in_specs[-3] = in_vmem
    def kernel(*refs):
        fold_kernel(groups, list(mine), list(theirs), first, last, *refs)

    return pl.pallas_call(
        kernel,
        out_shape=shapes,
        in_specs=in_specs,
        out_specs=[ANY, ANY, in_vmem],
        scratch_shapes=scratch,
        input_output_aliases=aliases,
        compiler_params=params(FOLD_VMEM),
        cost_estimate=pl.CostEstimate(
            flops=0, bytes_accessed=1 << 20,
            transcendentals=0,
        ),
        name="fold",
    )(*operands)


def per_device(deltas, outer_weights, momentum, tokens, key_cot):
    x, zh, zl, y, c = [lax.axis_index(a) for a in AXES]
    z = zh * 2 + zl
    way = 1 - 2 * c
    at = jnp.stack([x, z, y, zl, c]).astype(jnp.int32)
    blocks = deltas[0]

    tokens_theirs = swap_core(other_half(at, tokens))
    cot_theirs = swap_core(key_cot)

    def grads(which, tokens_theirs, *arrived):
        blocks = [
            (zl if half else 1 - zl) * 4 + ((y - way * (s + 1) + 8) & 3)
            for half, s in which
        ]
        return grad_blocks(
            blocks, c, tokens, tokens_theirs, key_cot, cot_theirs, arrived
        )

    def add(*parts):
        total = parts[0].astype(F32)
        for part in parts[1:]:
            total = total + part.astype(F32)
        return total

    by_x = blocks.reshape(4, 2, 64, COLS)
    got = []
    for d in (2, 1, 3):
        piece = lax.dynamic_index_in_dim(by_x, (x + d) & 3, 0, False)
        got.append(permute(piece, lambda px, pz, py, pc: (px + d, pz, py, pc)))
    first, first_b = grads([(0, 0), (1, 0)], tokens_theirs)
    *got, first, first_b = lax.optimization_barrier((*got, first, first_b[0]))
    arrived = ring_y(first)
    part = add(lax.dynamic_index_in_dim(by_x, x, 0, False), *got)
    crossing = lax.dynamic_index_in_dim(part, 1 - zh, 0, False).astype(BF)
    crossing = permute(crossing, lambda px, pz, py, pc: (px, pz + 2, py, pc))
    summed = add(lax.dynamic_index_in_dim(part, zh, 0, False), crossing)
    mean_delta = summed / 8
    moment_next = MOMENTUM_RATE * momentum[0, 0] + mean_delta
    outer_next = outer_weights[0, 0] - OUTER_RATE * (
        mean_delta + MOMENTUM_RATE * moment_next
    )
    owned = outer_next.astype(BF)

    def short_way(value, d):
        return permute(
            value,
            lambda px, pz, py, pc: (px - d * pc, pz - d * (1 - pc), py, pc),
        )

    def long_way(value, d):
        return permute(
            value,
            lambda px, pz, py, pc: (px + d * (1 - pc), pz + d * pc, py, pc),
        )

    def in_order(parts, here):
        whole = jnp.zeros((2, 4, 2, 64, COLS), BF)
        for d, part in enumerate(parts):
            whole = lax.dynamic_update_slice_in_dim(
                whole, part[:, None], (here + d) & 3, 1
            )
        return whole

    other, arrived = lax.optimization_barrier((swap_core(owned), arrived))
    both = jnp.where(c == 0, jnp.stack([owned, other]), jnp.stack([other, owned]))
    near = permute(both, lambda px, pz, py, pc: (px, pz, py - 1 + 2 * pc, pc))
    far = permute(both, lambda px, pz, py, pc: (px, pz, py + 2 * pc, pc))
    c0 = jnp.stack([far, near])
    c0, first_b, late = lax.optimization_barrier((c0, first_b, tokens_theirs))
    arrived_b = ring_y(first_b)
    (second,) = grads([(0, 1)], late, arrived)
    parts = [short_way(c0, d) for d in (1, 2, 3)]
    arrived = ring_y(second)
    c1 = in_order([c0] + parts, jnp.where(c == 0, z, x))
    c1, late = lax.optimization_barrier((c1, late))
    (third,) = grads([(0, 2)], late, arrived)
    third, late = lax.optimization_barrier((third, late))
    second_b, rest = grads([(1, 1), (0, 3), (1, 2), (1, 3)], late)

    mine, theirs = {0: c1}, {0: swap_core(c1)}
    mine[1], mine[3] = long_way(c1, 1), long_way(c1, -1)

    def fold_of(groups, keys, carry, last):
        return fold(
            at, tokens, key_cot, groups,
            {k: mine[k] for k in keys}, {k: theirs[k] for k in keys}, carry, last,
        )

    carry = fold_of([("x", 0, 0), ("x", 0, 1)], [0], None, False)
    arrived = ring_y(third)
    mine[1], mine[3], arrived, arrived_b, rest, *carry = lax.optimization_barrier(
        (mine[1], mine[3], arrived, arrived_b, rest, *carry)
    )
    mine[2, 0] = long_way(mine[1][0], 1)
    mine[2, 1] = long_way(mine[3][1], -1)
    theirs[1], theirs[3] = swap_core(mine[1]), swap_core(mine[3])
    crossed = add(rest[0], arrived).astype(BF)
    crossed = [
        permute(half, lambda px, pz, py, pc: (px, pz ^ 1, py, pc))
        for half in (crossed[:192], crossed[192:])
    ]
    arrived_b = ring_y(add(second_b, arrived_b).astype(BF))
    groups = [("x", s, dy) for s in (1, 3) for dy in range(2)]
    groups += [("z", (1, 3), dy, p) for dy in range(2) for p in range(2)]
    carry = fold_of(groups, [1, 3], carry, False)
    mine[2, 0], mine[2, 1], arrived_b, crossed[0], *carry = lax.optimization_barrier(
        (mine[2, 0], mine[2, 1], arrived_b, crossed[0], *carry)
    )
    theirs[2, 0], theirs[2, 1] = swap_core(mine[2, 0]), swap_core(mine[2, 1])
    arrived_b = ring_y(add(rest[1], arrived_b).astype(BF))
    groups = [("x", 2, dy) for dy in range(2)]
    groups += [("z", (0, 2), dy, p) for dy in range(2) for p in range(2)]
    grad_tokens, shard_weights, keys_out = fold_of(
        groups, [0, (2, 0), (2, 1)], carry, True
    )
    arrived_b, *crossed, keys_out = lax.optimization_barrier(
        (arrived_b, *crossed, keys_out)
    )
    grad_shard = add(rest[2], arrived_b, jnp.concatenate(crossed))
    shard_weights = shard_weights.reshape(512, COLS)

    return (
        outer_next[None, None],
        moment_next[None, None],
        shard_weights,
        keys_out,
        grad_tokens,
        grad_shard[None],
    )


def solution(mesh):
    fine = Mesh(mesh.devices.reshape(SIZES), AXES)
    rep, fsdp = ("x", "zh"), ("zl", "y", "c")
    return jax.shard_map(
        per_device,
        mesh=fine,
        in_specs=(
            P(rep, fsdp, None),
            P(fsdp, rep, None, None),
            P(fsdp, rep, None, None),
            P(AXES, None),
            P(AXES, None),
        ),
        out_specs=(
            P(fsdp, rep, None, None),
            P(fsdp, rep, None, None),
            P(fsdp, None),
            P(AXES, None),
            P(AXES, None),
            P(rep, fsdp, None),
        ),
        check_vma=False,
    )
```

```python
import functools
import itertools

import jax
import jax.numpy as jnp
import numpy as np
from jax import lax
from jax.experimental import pallas as pl
from jax.experimental.pallas import tpu as pltpu
from jax.sharding import Mesh, PartitionSpec as P

MOMENTUM_RATE = 0.9
OUTER_RATE = 0.7
AXES = ("x", "zh", "zl", "y", "c")
SIZES = (4, 2, 2, 4, 2)
TOK = 512
D = 8192
COLS = 1024
SCALE = D ** (-0.5)
VMEM = 44 * 1024 * 1024
FOLD_VMEM = 28 * 1024 * 1024
ANY = pl.BlockSpec(memory_space=pl.ANY)
BF = jnp.bfloat16
F32 = jnp.float32


def permute(value, to):
    pairs = []
    for x, zh, zl, y, c in itertools.product(*[range(n) for n in SIZES]):
        tx, tz, ty, tc = to(x, zh * 2 + zl, y, c)
        tz = tz % 4
        target = (tx % 4, tz // 2, tz % 2, ty % 4, tc % 2)
        pairs.append(
            (
                int(np.ravel_multi_index((x, zh, zl, y, c), SIZES)),
                int(np.ravel_multi_index(target, SIZES)),
            )
        )
    return lax.ppermute(value, AXES, pairs)


def swap_core(value):
    return permute(value, lambda x, z, y, c: (x, z, y, 1 - c))


def ring_y(value):
    return permute(value, lambda x, z, y, c: (x, z, y + 1 - 2 * c, c))


def params(limit=VMEM):
    return pltpu.CompilerParams(vmem_limit_bytes=limit)


def half_kernel(at, tokens, out, held, in_sem, out_sem):
    c = at[4]
    loads = [
        pltpu.make_async_copy(
            tokens.at[:, pl.ds(pl.multiple_of((2 * g + 1 - c) * 512, 512), 512)],
            held.at[:, pl.ds(g * 512, 512)],
            in_sem.at[g],
        )
        for g in range(8)
    ]
    stores = [
        pltpu.make_async_copy(
            held.at[:, pl.ds(g * 512, 512)],
            out.at[:, pl.ds(g * 512, 512)],
            out_sem.at[g],
        )
        for g in range(8)
    ]
    for load in loads:
        load.start()
    for load, store in zip(loads, stores):
        load.wait()
        store.start()
    for store in stores:
        store.wait()


def other_half(at, tokens):
    return pl.pallas_call(
        half_kernel,
        out_shape=jax.ShapeDtypeStruct((TOK, D // 2), BF),
        in_specs=[pl.BlockSpec(memory_space=pltpu.SMEM), ANY],
        out_specs=ANY,
        scratch_shapes=[
            pltpu.VMEM((TOK, D // 2), BF),
            pltpu.SemaphoreType.DMA((8,)),
            pltpu.SemaphoreType.DMA((8,)),
        ],
        compiler_params=params(),
        cost_estimate=pl.CostEstimate(
            flops=0, bytes_accessed=2 * TOK * D, transcendentals=0
        ),
        name="half",
    )(at, tokens)


def grad_kernel(adds, blocks, mine, theirs, cot, cot_theirs, *refs):
    arrived, (out, *rest) = refs[:adds], refs[adds:]
    dims = (((0,), (0,)), ((), ()))
    total = lax.dot_general(mine[...], cot[...], dims, preferred_element_type=F32)
    total += lax.dot_general(
        theirs[...], cot_theirs[...], dims, preferred_element_type=F32
    )
    total = total * SCALE

    @pl.when(pl.program_id(0) == 0)
    def _():
        first = total
        for part in arrived:
            first = first + part[...].astype(F32)
        out[...] = first.astype(BF)

    for more in rest:

        @pl.when(pl.program_id(0) > 0)
        def _(more=more):
            more[0] = total.astype(BF)


def grad_blocks(blocks, core, tokens, tokens_theirs, cot, cot_theirs, arrived):
    count = len(blocks)
    table = jnp.stack([2 * g + core for g in blocks] + blocks).astype(jnp.int32)
    whole = pl.BlockSpec((TOK, COLS), lambda m, b: (0, 0))
    return pl.pallas_call(
        functools.partial(grad_kernel, len(arrived)),
        out_shape=[
            jax.ShapeDtypeStruct((512, COLS), BF),
            jax.ShapeDtypeStruct((count - 1, 512, COLS), BF),
        ][: min(count, 2)],
        grid_spec=pltpu.PrefetchScalarGridSpec(
            num_scalar_prefetch=1,
            grid=(count,),
            in_specs=[
                pl.BlockSpec((TOK, 512), lambda m, b: (0, b[m])),
                pl.BlockSpec((TOK, 512), lambda m, b: (0, b[count + m])),
                whole,
                whole,
            ]
            + [whole] * len(arrived),
            out_specs=[
                whole,
                pl.BlockSpec((1, 512, COLS), lambda m, b: (jnp.maximum(m - 1, 0), 0, 0)),
            ][: min(count, 2)],
        ),
        compiler_params=params(),
        cost_estimate=pl.CostEstimate(
            flops=count * 4 * TOK * 512 * COLS,
            bytes_accessed=(count * 2 + 2) << 20,
            transcendentals=0,
        ),
        name="grad",
    )(table, tokens, tokens_theirs, cot, cot_theirs, *arrived)


OFFSETS = (0, -1, 2, 1)


def fold_kernel(groups, mine, theirs, first, last, *refs):
    refs = list(refs)
    at, tokens, cot = refs[:3]
    refs = refs[3:]
    mine = {key: refs.pop(0) for key in mine}
    theirs = {key: refs.pop(0) for key in theirs}
    if not first:
        acc_in, _, _ = refs.pop(0), refs.pop(0), refs.pop(0)
    grad_out, weights_out, key_out = refs.pop(0), refs.pop(0), refs.pop(0)
    w, tok, grad, cot_v, w_sem, tok_sem, out_sem, own_sem, cot_sem = refs[:9]
    acc = refs[9] if last else key_out
    x, z, y, c = at[0], at[1], at[2], at[4]

    def part(held, s, dy):
        return held[s, dy] if (s, dy) in held else held[s].at[dy]

    def x_of(s):
        return (x + OFFSETS[s] + 4) & 3

    def z_of(s):
        return (z + OFFSETS[s] + 4) & 3

    def columns_of(group):
        if group[0] == "x":
            _, s, dy = group
            return [
                (
                    (zl * 8 + ((y + dy) & 3) * 2 + p) * 512 + x_of(s) * 128,
                    (zl * 2 + p) * 128,
                    128,
                )
                for zl in range(2)
                for p in range(2)
            ]
        _, (s, t), dy, p = group
        return [(((z_of(s) & 1) * 8 + ((y + 2 + dy) & 3) * 2 + p) * 512, 0, 512)]

    def load_weights(group, slot):
        def start(held):
            if group[0] == "x":
                _, s, dy = group
                for zl, zh in itertools.product(range(2), range(2)):
                    pltpu.make_async_copy(
                        part(held, s, dy).at[zh * 2 + zl],
                        w.at[slot, pl.ds(zl * 2, 2), zh],
                        w_sem.at[slot],
                    ).start()
            else:
                _, pair, dy, p = group
                for s in pair:
                    pltpu.make_async_copy(
                        part(held, s, dy).at[:, p],
                        w.at[slot, :, z_of(s) >> 1],
                        w_sem.at[slot],
                    ).start()

        here = 0 if group[0] == "x" else 1
        @pl.when(c == here)
        def _():
            start(mine)

        @pl.when(c != here)
        def _():
            start(theirs)

    count = len(groups)

    def loads(i):
        slot = i % 3
        load_weights(groups[i], slot)
        for a, b, n in columns_of(groups[i]):
            pltpu.make_async_copy(
                tokens.at[:, pl.ds(pl.multiple_of(a, 128), n)],
                tok.at[slot, :, pl.ds(b, n)],
                tok_sem.at[slot],
            ).start()

    def holds_own(group):
        return group[0] == "x" and group[2] == 0

    def weights_store(i):
        slot = i % 3
        return pltpu.make_async_copy(
            w.at[slot, (z & 1) * 2 + c],
            weights_out.at[x_of(groups[i][1])],
            own_sem.at[slot],
        )

    def stores(i):
        slot = i % 3
        for a, b, n in columns_of(groups[i]):
            pltpu.make_async_copy(
                grad.at[slot, :, pl.ds(b, n)],
                grad_out.at[:, pl.ds(pl.multiple_of(a, 128), n)],
                out_sem.at[slot],
            ).start()

    def whole(buffer, sem, slot):
        return pltpu.make_async_copy(buffer.at[slot], buffer.at[slot], sem.at[slot])

    cot_copy = pltpu.make_async_copy(cot, cot_v, cot_sem)
    cot_copy.start()
    loads(0)
    loads(1)
    if first:
        acc[...] = jnp.zeros_like(acc)
    else:
        acc[...] = acc_in[...]
    cot_copy.wait()

    @pl.loop(0, count)
    def _(i):
        slot = lax.rem(i, 3)
        for k in range(2, count):

            @pl.when(i + 2 == k)
            def _(k=k):
                loads(k)

        whole(w, w_sem, slot).wait()
        for k in range(count):
            if holds_own(groups[k]):

                @pl.when(i == k)
                def _(k=k):
                    weights_store(k).start()

        @pl.when(i >= 3)
        def _():
            whole(grad, out_sem, slot).wait()

        rows = w[slot].reshape(512, COLS)
        out = lax.dot_general(
            cot_v[...], rows, (((1,), (1,)), ((), ())), preferred_element_type=F32
        )
        grad[slot] = (out * SCALE).astype(BF)
        for k in range(count):

            @pl.when(i == k)
            def _(k=k):
                stores(k)

        whole(tok, tok_sem, slot).wait()
        acc[...] += jnp.dot(tok[slot], rows, preferred_element_type=F32)
        for k in range(count):
            if holds_own(groups[k]):

                @pl.when(i == k)
                def _(k=k):
                    weights_store(k).wait()

    if last:
        key_out[...] = (acc[...] * SCALE).astype(BF)
    for i in range(max(count - 3, 0), count):
        whole(grad, out_sem, i % 3).wait()


def fold(at, tokens, cot, groups, mine, theirs, carry, last):
    first = carry is None
    operands = [at, tokens, cot, *mine.values(), *theirs.values()]
    aliases = {}
    if not first:
        operands += [carry[2]]
        aliases = {len(operands): 0, len(operands) + 1: 1}
        operands += carry[:2]
    shapes = [
        jax.ShapeDtypeStruct((TOK, D), BF),
        jax.ShapeDtypeStruct((4, 2, 64, COLS), BF),
        jax.ShapeDtypeStruct((TOK, COLS), BF if last else F32),
    ]
    dma = pltpu.SemaphoreType.DMA
    scratch = [
        pltpu.VMEM((3, 4, 2, 64, COLS), BF),
        pltpu.VMEM((3, TOK, 512), BF),
        pltpu.VMEM((3, TOK, 512), BF),
        pltpu.VMEM((TOK, COLS), BF),
        dma((3,)),
        dma((3,)),
        dma((3,)),
        dma((3,)),
        dma(()),
    ]
    if last:
        scratch += [pltpu.VMEM((TOK, COLS), F32)]
    in_vmem = pl.BlockSpec(memory_space=pltpu.VMEM)
    in_specs = [pl.BlockSpec(memory_space=pltpu.SMEM)] + [ANY] * (len(operands) - 1)
    if not first:
        in_specs[-3] = in_vmem
    def kernel(*refs):
        fold_kernel(groups, list(mine), list(theirs), first, last, *refs)

    return pl.pallas_call(
        kernel,
        out_shape=shapes,
        in_specs=in_specs,
        out_specs=[ANY, ANY, in_vmem],
        scratch_shapes=scratch,
        input_output_aliases=aliases,
        compiler_params=params(FOLD_VMEM),
        cost_estimate=pl.CostEstimate(
            flops=0, bytes_accessed=1 << 20,
            transcendentals=0,
        ),
        name="fold",
    )(*operands)


def per_device(deltas, outer_weights, momentum, tokens, key_cot):
    x, zh, zl, y, c = [lax.axis_index(a) for a in AXES]
    z = zh * 2 + zl
    way = 1 - 2 * c
    at = jnp.stack([x, z, y, zl, c]).astype(jnp.int32)
    blocks = deltas[0]

    tokens_theirs = swap_core(other_half(at, tokens))
    cot_theirs = swap_core(key_cot)

    def grads(which, tokens_theirs, *arrived):
        blocks = [
            (zl if half else 1 - zl) * 4 + ((y - way * (s + 1) + 8) & 3)
            for half, s in which
        ]
        return grad_blocks(
            blocks, c, tokens, tokens_theirs, key_cot, cot_theirs, arrived
        )

    def add(*parts):
        total = parts[0].astype(F32)
        for part in parts[1:]:
            total = total + part.astype(F32)
        return total

    by_x = blocks.reshape(4, 2, 64, COLS)
    got = []
    for d in (2, 1, 3):
        piece = lax.dynamic_index_in_dim(by_x, (x + d) & 3, 0, False)
        got.append(permute(piece, lambda px, pz, py, pc: (px + d, pz, py, pc)))
    first, first_b = grads([(0, 0), (1, 0)], tokens_theirs)
    *got, first, first_b = lax.optimization_barrier((*got, first, first_b[0]))
    arrived = ring_y(first)
    part = add(lax.dynamic_index_in_dim(by_x, x, 0, False), *got)
    crossing = lax.dynamic_index_in_dim(part, 1 - zh, 0, False).astype(BF)
    crossing = permute(crossing, lambda px, pz, py, pc: (px, pz + 2, py, pc))
    summed = add(lax.dynamic_index_in_dim(part, zh, 0, False), crossing)
    mean_delta = summed / 8
    moment_next = MOMENTUM_RATE * momentum[0, 0] + mean_delta
    outer_next = outer_weights[0, 0] - OUTER_RATE * (
        mean_delta + MOMENTUM_RATE * moment_next
    )
    owned = outer_next.astype(BF)

    def short_way(value, d):
        return permute(
            value,
            lambda px, pz, py, pc: (px - d * pc, pz - d * (1 - pc), py, pc),
        )

    def long_way(value, d):
        return permute(
            value,
            lambda px, pz, py, pc: (px + d * (1 - pc), pz + d * pc, py, pc),
        )

    def in_order(parts, here):
        whole = jnp.zeros((2, 4, 2, 64, COLS), BF)
        for d, part in enumerate(parts):
            whole = lax.dynamic_update_slice_in_dim(
                whole, part[:, None], (here + d) & 3, 1
            )
        return whole

    other, arrived = lax.optimization_barrier((swap_core(owned), arrived))
    both = jnp.where(c == 0, jnp.stack([owned, other]), jnp.stack([other, owned]))
    near = permute(both, lambda px, pz, py, pc: (px, pz, py - 1 + 2 * pc, pc))
    far = permute(both, lambda px, pz, py, pc: (px, pz, py + 2 * pc, pc))
    c0 = jnp.stack([far, near])
    c0, first_b, late = lax.optimization_barrier((c0, first_b, tokens_theirs))
    arrived_b = ring_y(first_b)
    (second,) = grads([(0, 1)], late, arrived)
    parts = [short_way(c0, d) for d in (1, 2, 3)]
    arrived = ring_y(second)
    c1 = in_order([c0] + parts, jnp.where(c == 0, z, x))
    c1, late = lax.optimization_barrier((c1, late))
    (third,) = grads([(0, 2)], late, arrived)
    third, late = lax.optimization_barrier((third, late))
    second_b, rest = grads([(1, 1), (0, 3), (1, 2), (1, 3)], late)

    mine, theirs = {0: c1}, {0: swap_core(c1)}
    mine[1], mine[3] = long_way(c1, 1), long_way(c1, -1)

    def fold_of(groups, keys, carry, last):
        return fold(
            at, tokens, key_cot, groups,
            {k: mine[k] for k in keys}, {k: theirs[k] for k in keys}, carry, last,
        )

    carry = fold_of([("x", 0, 0), ("x", 0, 1)], [0], None, False)
    arrived = ring_y(third)
    summed_b = add(second_b, arrived_b).astype(BF)
    mine[1], mine[3], arrived, summed_b, rest, *carry = lax.optimization_barrier(
        (mine[1], mine[3], arrived, summed_b, rest, *carry)
    )
    mine[2, 0] = long_way(mine[1][0], 1)
    mine[2, 1] = long_way(mine[3][1], -1)
    theirs[1], theirs[3] = swap_core(mine[1]), swap_core(mine[3])
    crossed = add(rest[0], arrived).astype(BF)
    crossed = [
        permute(half, lambda px, pz, py, pc: (px, pz ^ 1, py, pc))
        for half in (crossed[:192], crossed[192:])
    ]
    arrived_b = ring_y(summed_b)
    groups = [("x", s, dy) for s in (1, 3) for dy in range(2)]
    groups += [("z", (1, 3), dy, p) for dy in range(2) for p in range(2)]
    carry = fold_of(groups, [1, 3], carry, False)
    mine[2, 0], mine[2, 1], arrived_b, crossed[0], *carry = lax.optimization_barrier(
        (mine[2, 0], mine[2, 1], arrived_b, crossed[0], *carry)
    )
    theirs[2, 0], theirs[2, 1] = swap_core(mine[2, 0]), swap_core(mine[2, 1])
    arrived_b = ring_y(add(rest[1], arrived_b).astype(BF))
    groups = [("x", 2, dy) for dy in range(2)]
    groups += [("z", (0, 2), dy, p) for dy in range(2) for p in range(2)]
    grad_tokens, shard_weights, keys_out = fold_of(
        groups, [0, (2, 0), (2, 1)], carry, True
    )
    arrived_b, *crossed, keys_out = lax.optimization_barrier(
        (arrived_b, *crossed, keys_out)
    )
    grad_shard = add(rest[2], arrived_b, jnp.concatenate(crossed))
    shard_weights = shard_weights.reshape(512, COLS)

    return (
        outer_next[None, None],
        moment_next[None, None],
        shard_weights,
        keys_out,
        grad_tokens,
        grad_shard[None],
    )


def solution(mesh):
    fine = Mesh(mesh.devices.reshape(SIZES), AXES)
    rep, fsdp = ("x", "zh"), ("zl", "y", "c")
    return jax.shard_map(
        per_device,
        mesh=fine,
        in_specs=(
            P(rep, fsdp, None),
            P(fsdp, rep, None, None),
            P(fsdp, rep, None, None),
            P(AXES, None),
            P(AXES, None),
        ),
        out_specs=(
            P(fsdp, rep, None, None),
            P(fsdp, rep, None, None),
            P(fsdp, None),
            P(AXES, None),
            P(AXES, None),
            P(rep, fsdp, None),
        ),
        check_vma=False,
    )
```
